32 devices in a mesh: seq: 8 (over y, x, core), tp: 4 (over z).
Axes of the slice: x: 2, y: 2, z: 4, core: 2. Of those that a mesh axis runs over, the one named last changes fastest.
Arguments:
- short_inputs: bfloat16 [4, 2560, 1280], P(None, 'seq'), may hold values from -8 to 8
- long_inputs: bfloat16 [4, 12, 1280], replicated, may hold values from -8 to 8
- short_keys: bfloat16 [2560, 16, 1280], P('seq', None, 'tp'), may hold values from -6 to 6
- short_values: bfloat16 [2560, 16, 1280], P('seq', None, 'tp'), may hold values from -6 to 6
- long_keys: bfloat16 [12, 128, 1280], P(None, 'seq', 'tp'), may hold values from -6 to 6
- long_values: bfloat16 [12, 128, 1280], P(None, 'seq', 'tp'), may hold values from -6 to 6
- short_lengths: int32 [2560], P('seq'), may hold values from 1 to 16, as said below
- long_lengths: int32 [12], replicated, may hold values from 32 to 128, as said below
- attn_gain: float32 [1280], replicated, may hold values from 0.1 to 1.9
- mlp_gain: float32 [1280], replicated, may hold values from 0.1 to 1.9
- query_scale: float32 [16, 80], P('tp'), may hold values from 1 to 40, as said below
- q_weight: bfloat16 [1280, 1280], P(None, 'tp'), may hold values from -0.15625 to 0.15625
- k_weight: bfloat16 [1280, 1280], P(None, 'tp'), may hold values from -0.15625 to 0.15625
- v_weight: bfloat16 [1280, 1280], P(None, 'tp'), may hold values from -0.15625 to 0.15625
- o_weight: bfloat16 [1280, 1280], P('tp'), may hold values from -0.15625 to 0.15625
- up_weight: bfloat16 [1280, 1280], P(None, 'tp'), may hold values from -0.15625 to 0.15625
- down_weight: bfloat16 [1280, 1280], P('tp'), may hold values from -0.15625 to 0.15625
Outputs:
- short_outputs: bfloat16 [4, 2560, 1280], P(None, 'seq', 'tp')
- long_outputs: bfloat16 [4, 12, 1280], P(None, None, 'tp')
The draws below stay inside these ranges and needn't reach their ends.
Inputs may be any that keep to these rules, and one draw needn't show every extreme that they name: `short_lengths`: some short request fills all 16 slots. `long_lengths`: some long request fills all 128 slots. `query_scale`: positive scales.
All inputs are finite; a program needn't handle non-finite values.
Results may differ from the reference program's by a relative error of at most 0.012.
The reference program's roundings to bfloat16 on the way count: a program that leaves them out, or rounds other values in their place, can miss the bound.
Values may be sent and summed in bfloat16 or wider, within the bound.
No kernel may reach another device: no remote copies, remote signals or barrier semaphores. Data moves between devices by JAX's collectives and lax.ppermute only.
A program may use at most 128 MiB of HBM per device.

```python
import math
import jax
import jax.numpy as jnp
from jax import lax

D = 1280
H = 16
HD = 80
FF = 1280
STEPS = 4
SHORT_CAP = 16
B_LONG = 12
B_SHORT = 2560
LONG_CAP = 128


def feature_rows(key, row_shape):
    base_key, jitter_key = jax.random.split(key)
    position = jnp.arange(D, dtype=jnp.float32) / (D - 1)
    jitter = jnp.exp(jax.random.uniform(jitter_key, (D,), jnp.float32, math.log(0.8), math.log(1.25)))
    ramp = 0.5 * jnp.exp(math.log(3.0) * position)
    noise = jax.random.normal(base_key, row_shape + (D,), jnp.float32)
    return jnp.clip(noise * ramp * jitter, -8.0, 8.0)


def draw_short_inputs(key, part):
    return feature_rows(jax.random.fold_in(key, 41), (STEPS, B_SHORT)).astype(jnp.bfloat16)


def draw_long_inputs(key, part):
    return feature_rows(jax.random.fold_in(key, 43), (STEPS, B_LONG)).astype(jnp.bfloat16)


def draw_short_lengths(key, part):
    first_key, second_key = jax.random.split(jax.random.fold_in(key, 11))
    values = jax.random.randint(first_key, (B_SHORT,), 1, SHORT_CAP + 1)
    spot_index = jax.random.randint(second_key, (), 0, B_SHORT)
    return values.at[spot_index].set(SHORT_CAP).astype(jnp.int32)


def draw_long_lengths(key, part):
    first_key, second_key = jax.random.split(jax.random.fold_in(key, 23))
    values = jax.random.randint(first_key, (B_LONG,), LONG_CAP // 4, LONG_CAP + 1)
    spot_index = jax.random.randint(second_key, (), 0, B_LONG)
    return values.at[spot_index].set(LONG_CAP).astype(jnp.int32)


def draw_query_scale(key, part):
    uniform_draw = jax.random.uniform(jax.random.fold_in(key, 37), (H, HD), jnp.float32)
    high_log = math.log(6.0)
    return jnp.exp(high_log * uniform_draw).astype(jnp.float32)


def levels(stream_key, shape, cuts, smallest, largest):
    gain, own = 1.0, jax.random.fold_in(stream_key, 6)
    for axis_at, parts in cuts:
        draws = jnp.exp(jax.random.uniform(jax.random.fold_in(own, axis_at), (parts,), jnp.float32, smallest / len(cuts), largest / len(cuts)))
        gain = gain * jnp.repeat(draws, shape[axis_at] // parts).reshape([-1 if axis == axis_at else 1 for axis in range(len(shape))])
    return gain


def gaussian(own_key, extent, scale, most, cuts=(), kind=jnp.bfloat16):
    values = scale * jax.random.normal(own_key, extent, jnp.float32)
    if cuts:
        values = values * levels(own_key, extent, cuts, -0.22, 0.18)
    return jnp.clip(values, -most, most).astype(kind)


def setup_inputs(seed: int = 0) -> dict:
    seeds = jax.random.split(jax.random.key(seed), 18)
    short_inputs = draw_short_inputs(jax.random.fold_in(seeds[17], 71), 0)
    long_inputs = draw_long_inputs(jax.random.fold_in(seeds[17], 71), 0)
    short_keys = gaussian(seeds[2], (B_SHORT, SHORT_CAP, H * HD), 1.0, 6.0, ((0, 8), (2, 4)))
    short_values = gaussian(seeds[3], (B_SHORT, SHORT_CAP, H * HD), 1.0, 6.0, ((0, 8), (2, 4)))
    long_keys = gaussian(seeds[4], (B_LONG, LONG_CAP, H * HD), 1.0, 6.0, ((1, 8), (2, 4)))
    long_values = gaussian(seeds[5], (B_LONG, LONG_CAP, H * HD), 1.0, 6.0, ((1, 8), (2, 4)))
    short_lengths = draw_short_lengths(jax.random.fold_in(seeds[17], 71), 0)
    long_lengths = draw_long_lengths(jax.random.fold_in(seeds[17], 71), 0)
    attn_gain = jnp.clip(1.0 + 0.18 * jax.random.normal(seeds[8], (D,), jnp.float32), 0.1, 1.9)
    mlp_gain = jnp.clip(1.0 + 0.18 * jax.random.normal(seeds[9], (D,), jnp.float32), 0.1, 1.9)
    query_scale = draw_query_scale(jax.random.fold_in(seeds[17], 71), 0)
    q_weight = gaussian(seeds[11], (D, H * HD), D ** -0.5, 0.15625, ((1, 4),))
    k_weight = gaussian(seeds[12], (D, H * HD), D ** -0.5, 0.15625, ((1, 4),))
    v_weight = gaussian(seeds[13], (D, H * HD), D ** -0.5, 0.15625, ((1, 4),))
    o_weight = gaussian(seeds[14], (H * HD, D), (H * HD) ** -0.5, 0.15625, ((0, 4),))
    up_weight = gaussian(seeds[15], (D, FF), D ** -0.5, 0.15625, ((1, 4),))
    down_weight = gaussian(seeds[16], (FF, D), FF ** -0.5, 0.15625, ((0, 4),))
    return dict(short_inputs=short_inputs, long_inputs=long_inputs, short_keys=short_keys, short_values=short_values, long_keys=long_keys, long_values=long_values, short_lengths=short_lengths, long_lengths=long_lengths, attn_gain=attn_gain, mlp_gain=mlp_gain, query_scale=query_scale, q_weight=q_weight, k_weight=k_weight, v_weight=v_weight, o_weight=o_weight, up_weight=up_weight, down_weight=down_weight)


norm_eps = 1e-06
masked_fill = -1e+30

def rms_scale(matrix, gain_row):
    mean_square = lax.optimization_barrier(jnp.sum(matrix * matrix, axis=-1, keepdims=True)) / matrix.shape[-1]
    return matrix * lax.rsqrt(mean_square + norm_eps) * gain_row

def project_heads(flat_rows, weight, step_count, head_count):
    product = jnp.dot(flat_rows, weight, preferred_element_type=jnp.float32)
    return product.reshape(step_count, -1, head_count, product.shape[-1] // head_count)

def attend_group(queries, cache_keys, cache_values, lengths, new_keys, new_values):
    step_count = queries.shape[0]
    head_count, head_dim = (queries.shape[2], queries.shape[3])
    causal = jnp.arange(step_count)[None, :] <= jnp.arange(step_count)[:, None]

    def attend_one(request):
        own_queries, own_keys, own_values, length, own_new_keys, own_new_values = request
        keys_wide = own_keys.astype(jnp.float32).reshape(own_keys.shape[0], head_count, head_dim)
        values_wide = own_values.astype(jnp.float32).reshape(own_values.shape[0], head_count, head_dim)
        queries_wide = own_queries.astype(jnp.float32)
        cache_scores = jnp.einsum('shd,chd->shc', queries_wide, keys_wide)
        valid_slots = jnp.arange(own_keys.shape[0]) < length
        cache_scores = jnp.where(valid_slots, cache_scores, masked_fill)
        fresh_scores = jnp.einsum('shd,thd->sht', queries_wide, own_new_keys.astype(jnp.float32))
        fresh_mask = causal[:, None, :]
        fresh_scores = jnp.where(fresh_mask, fresh_scores, masked_fill)
        row_max = jnp.maximum(lax.optimization_barrier(jnp.max(cache_scores, axis=-1)), lax.optimization_barrier(jnp.max(fresh_scores, axis=-1)))
        cache_probs = jnp.where(valid_slots, jnp.exp(cache_scores - row_max[..., None]), 0.0)
        fresh_probs = jnp.where(fresh_mask, jnp.exp(fresh_scores - row_max[..., None]), 0.0)
        denominator = lax.optimization_barrier(jnp.sum(cache_probs, axis=-1)) + lax.optimization_barrier(jnp.sum(fresh_probs, axis=-1))
        cache_low = lax.optimization_barrier(cache_probs.astype(jnp.bfloat16)).astype(jnp.float32)
        fresh_low = lax.optimization_barrier(fresh_probs.astype(jnp.bfloat16)).astype(jnp.float32)
        weighted = jnp.einsum('shc,chd->shd', cache_low, values_wide)
        weighted = weighted + jnp.einsum('sht,thd->shd', fresh_low, own_new_values.astype(jnp.float32))
        return (weighted / denominator[..., None]).astype(jnp.bfloat16)
    stacked = lax.map(attend_one, (jnp.swapaxes(queries, 0, 1), cache_keys, cache_values, lengths, jnp.swapaxes(new_keys, 0, 1), jnp.swapaxes(new_values, 0, 1)))
    return jnp.swapaxes(stacked, 0, 1)

def reference(short_inputs, long_inputs, short_keys, short_values, long_keys, long_values, short_lengths, long_lengths, attn_gain, mlp_gain, query_scale, q_weight, k_weight, v_weight, o_weight, up_weight, down_weight):
    step_count, short_count, model_width = short_inputs.shape
    head_count, head_dim = query_scale.shape
    all_rows = jnp.concatenate([short_inputs, long_inputs], axis=1)
    flat_rows = all_rows.reshape(-1, model_width)
    normed = rms_scale(flat_rows.astype(jnp.float32), attn_gain).astype(jnp.bfloat16)
    queries = (project_heads(normed, q_weight, step_count, head_count) * query_scale * head_dim ** (-0.5)).astype(jnp.bfloat16)
    new_keys = project_heads(normed, k_weight, step_count, head_count).astype(jnp.bfloat16)
    new_values = project_heads(normed, v_weight, step_count, head_count).astype(jnp.bfloat16)
    short_out = attend_group(queries[:, :short_count], short_keys, short_values, short_lengths, new_keys[:, :short_count], new_values[:, :short_count])
    long_out = attend_group(queries[:, short_count:], long_keys, long_values, long_lengths, new_keys[:, short_count:], new_values[:, short_count:])
    attended = jnp.concatenate([short_out, long_out], axis=1).reshape(flat_rows.shape[0], -1)
    residual_mid = flat_rows.astype(jnp.float32) + jnp.dot(attended, o_weight, preferred_element_type=jnp.float32)
    normed_mid = rms_scale(residual_mid, mlp_gain).astype(jnp.bfloat16)
    hidden = jax.nn.silu(jnp.dot(normed_mid, up_weight, preferred_element_type=jnp.float32)).astype(jnp.bfloat16)
    output = residual_mid + jnp.dot(hidden, down_weight, preferred_element_type=jnp.float32)
    output = output.astype(jnp.bfloat16).reshape(step_count, -1, model_width)
    return (output[:, :short_count], output[:, short_count:])
```

```python
import functools

import jax
import jax.numpy as jnp
from jax import lax
from jax.experimental import pallas as pl
from jax.experimental.pallas import tpu as pltpu
from jax.sharding import PartitionSpec as P

norm_eps = 1e-06
masked_fill = -1e30
GROUP = 16
F32 = jnp.float32
BF16 = jnp.bfloat16
MIB = 1024 * 1024


def rms_scale(rows, gain_row):
    mean_square = jnp.sum(rows * rows, axis=-1, keepdims=True) / rows.shape[-1]
    return (rows * lax.rsqrt(mean_square + norm_eps) * gain_row).astype(BF16)


def dot(a, b):
    return jnp.dot(a, b, preferred_element_type=F32)


def dot_t(a, b):
    return lax.dot_general(a, b, (((1,), (1,)), ((), ())), preferred_element_type=F32)


def lane_heads(rows, width, heads):
    return lax.broadcasted_iota(jnp.int32, (rows, width), 1) // (width // heads)


def stack_heads(queries, heads):
    head_of = lane_heads(*queries.shape, heads)
    return jnp.concatenate([jnp.where(head_of == h, queries, jnp.zeros_like(queries)) for h in range(heads)], axis=0)


def pick_heads(stacked, heads, width):
    n = stacked.shape[0] // heads
    head_of = lane_heads(n, width, heads)
    picked = jnp.broadcast_to(stacked[:n], (n, width))
    for h in range(1, heads):
        picked = jnp.where(head_of == h, stacked[h * n : (h + 1) * n], picked)
    return picked


def slot_bias(lens, slots, columns):
    at = lax.broadcasted_iota(jnp.int32, (GROUP, columns), 1) - slots * lax.broadcasted_iota(jnp.int32, (GROUP, columns), 0)
    return jnp.where((at >= 0) & (at < lens), 0.0, masked_fill)


def fresh_bias(steps):
    n = steps * GROUP
    row = lax.broadcasted_iota(jnp.int32, (n, n), 0)
    col = lax.broadcasted_iota(jnp.int32, (n, n), 1)
    seen = (row % GROUP == col % GROUP) & (col // GROUP <= row // GROUP)
    return jnp.where(seen, 0.0, masked_fill)


def add_rows(scores, bias):
    reps = scores.shape[0] // bias.shape[0]
    return (scores.reshape(reps, *bias.shape) + bias[None]).reshape(scores.shape)


def pick_lens(len_row, base):
    lane = lax.broadcasted_iota(jnp.int32, (GROUP, len_row.shape[1]), 1)
    row = lax.broadcasted_iota(jnp.int32, (GROUP, len_row.shape[1]), 0)
    return jnp.sum(jnp.where(lane == base + row, len_row, 0), axis=1, keepdims=True)


def qkv_rows(normed, qw_ref, kw_ref, vw_ref, scale_row, inv):
    queries = (dot(normed, qw_ref[...]) * scale_row * inv).astype(BF16)
    return queries, dot(normed, kw_ref[...]).astype(BF16), dot(normed, vw_ref[...]).astype(BF16)


def scale_lanes(scale_ref):
    return jnp.concatenate([scale_ref[h : h + 1, :] for h in range(scale_ref.shape[0])], axis=1)


def long_kernel(at_ref, x_ref, k_ref, v_ref, len_ref, gain_ref, scale_ref, qw_ref, kw_ref, vw_ref, part_ref, q_ref, kn_ref, vn_ref, rows_ref):
    steps, count, model = x_ref.shape
    heads, head_dim = scale_ref.shape
    width = heads * head_dim
    slots = k_ref.shape[1]
    rows_ref[...] = jnp.zeros_like(rows_ref)
    for s in range(steps):
        rows_ref[s * GROUP : s * GROUP + count, :] = x_ref[s].astype(F32)
    normed = rms_scale(rows_ref[...], gain_ref[...])
    q, kn, vn = qkv_rows(normed, qw_ref, kw_ref, vw_ref, scale_lanes(scale_ref), head_dim**-0.5)
    q_ref[...] = q
    kn_ref[...] = kn
    vn_ref[...] = vn
    lens = jnp.minimum(pick_lens(len_ref[...], 0) - at_ref[0] * slots, slots)
    keys = k_ref[...].reshape(count * slots, width)
    values = v_ref[...].reshape(count * slots, width)
    bias = slot_bias(lens, slots, count * slots)
    scores = add_rows(dot_t(stack_heads(q, heads), keys), bias)
    row_max = jnp.max(scores, axis=1, keepdims=True)
    probs = jnp.where(scores > 0.5 * masked_fill, jnp.exp(scores - row_max), 0.0)
    weight_sum = jnp.sum(probs, axis=1, keepdims=True)
    acc = pick_heads(dot(probs.astype(BF16), values), heads, width)
    n = steps * GROUP
    part_ref[:, :width] = acc
    lane = lax.broadcasted_iota(jnp.int32, (n, part_ref.shape[1] - width), 1)
    tail = jnp.zeros(lane.shape, F32)
    for h in range(heads):
        tail = jnp.where(lane == h, row_max[h * n : (h + 1) * n], tail)
        tail = jnp.where(lane == heads + h, weight_sum[h * n : (h + 1) * n], tail)
    part_ref[:, width:] = tail


def merge_long(my_seq, parts, held_ref, q, kn, vn, heads):
    n, width = q.shape
    for i, part in enumerate(parts):
        held_ref[my_seq ^ i] = part[...]
    scores = add_rows(dot_t(stack_heads(q, heads), kn), fresh_bias(n // GROUP))
    total_max = jnp.max(scores, axis=1, keepdims=True)

    def column(i, first):
        return jnp.concatenate([held_ref[i, :, first + h : first + h + 1] for h in range(heads)], axis=0)

    for i in range(len(parts)):
        total_max = jnp.maximum(total_max, column(i, width))
    probs = jnp.exp(scores - total_max)
    denom = jnp.sum(probs, axis=1, keepdims=True)
    acc = pick_heads(dot(probs.astype(BF16), vn), heads, width)
    for i in range(len(parts)):
        factor = jnp.exp(column(i, width) - total_max)
        denom = denom + factor * column(i, width + heads)
        acc = acc + held_ref[i, :, :width] * pick_heads(factor, heads, width)
    return (acc / pick_heads(denom, heads, width)).astype(BF16)


def short_kernel(n_parts, first, at_ref, x_ref, k_ref, v_ref, len_ref, gain_ref, scale_ref, qw_ref, kw_ref, vw_ref, *refs):
    parts, refs = refs[:n_parts], refs[n_parts:]
    if n_parts:
        longs, refs = refs[:3], refs[3:]
    steps, block, model = x_ref.shape
    heads, head_dim = scale_ref.shape
    width = heads * head_dim
    slots = k_ref.shape[1]
    outs, att_ref = refs[:steps], refs[steps]
    n = steps * GROUP
    i = pl.program_id(0)
    normed = rms_scale(x_ref[...].reshape(steps * block, model).astype(F32), gain_ref[...])
    q, kn, vn = qkv_rows(normed, qw_ref, kw_ref, vw_ref, scale_lanes(scale_ref), head_dim**-0.5)
    late = fresh_bias(steps)
    for sub in range(block // GROUP):
        lo, hi = sub * GROUP, (sub + 1) * GROUP

        def take(rows):
            return jnp.concatenate([rows[s * block + lo : s * block + hi] for s in range(steps)], axis=0)

        keys = k_ref[lo:hi].reshape(GROUP * slots, width)
        values = v_ref[lo:hi].reshape(GROUP * slots, width)
        lens = pick_lens(len_ref[...], first + i * block + lo)
        stacked = stack_heads(take(q), heads)
        scores = add_rows(dot_t(stacked, keys), slot_bias(lens, slots, GROUP * slots))
        fresh = add_rows(dot_t(stacked, take(kn)), late)
        row_max = jnp.maximum(jnp.max(scores, axis=1, keepdims=True), jnp.max(fresh, axis=1, keepdims=True))
        probs = jnp.exp(scores - row_max)
        fresh_probs = jnp.exp(fresh - row_max)
        denom = jnp.sum(probs, axis=1, keepdims=True) + jnp.sum(fresh_probs, axis=1, keepdims=True)
        weighted = dot(probs.astype(BF16), values) + dot(fresh_probs.astype(BF16), take(vn))
        out = (pick_heads(weighted, heads, width) / pick_heads(denom, heads, width)).astype(BF16)
        start = pl.multiple_of(i * block + lo, GROUP)
        for s in range(steps):
            att_ref[s, pl.ds(start, GROUP), :] = out[s * GROUP : (s + 1) * GROUP]

    @pl.when(i == pl.num_programs(0) - 1)
    def _():
        half = att_ref.shape[1] // 2
        if n_parts:
            long_ref, held_ref = refs[steps + 1], refs[steps + 2]
            merged = merge_long(at_ref[0], parts, held_ref, longs[0][...], longs[1][...], longs[2][...], heads)
            for s in range(steps):
                long_ref[s] = merged[s * GROUP : (s + 1) * GROUP]
        for k in range(steps):
            rows = att_ref[at_ref[1] ^ k]
            outs[k][:half, :] = jnp.concatenate([rows[:half], rows[half:]], axis=1)
            if n_parts:
                mine = long_ref[at_ref[1] ^ k]
                outs[k][half:, :] = jnp.concatenate([mine, jnp.zeros_like(mine)], axis=1)


def pack_kernel(at_ref, o_ref, up_ref, down_ref, out_ref):
    rows = o_ref.shape[0]
    out_ref[:rows, :] = o_ref[...]
    out_ref[rows : 2 * rows, :] = jnp.concatenate([up_ref[:rows, :], up_ref[rows:, :]], axis=1)
    out_ref[2 * rows :, :] = down_ref[...]


def unpack_kernel(tp, at_ref, own_o, own_up, own_down, *refs):
    o_ref, up_ref, down_ref = refs[-3:]
    width = own_o.shape[0]
    rows, lanes = refs[0].shape[0] // 3, refs[0].shape[1]
    mine = at_ref[0] % 8
    o_ref[:width, :] = own_o[...]
    up_ref[:, :width] = own_up[...]
    down_ref[:width, :] = own_down[...]
    for k in range(1, tp):
        for m in range(8):
            piece_ref = refs[(k - 1) * 8 + m]
            piece = mine ^ m
            row = pl.multiple_of(k * width + (piece // 2) * rows, 16)
            lane = pl.multiple_of((piece % 2) * lanes, 128)
            o_ref[pl.ds(row, rows), pl.ds(lane, lanes)] = piece_ref[:rows, :]
            down_ref[pl.ds(row, rows), pl.ds(lane, lanes)] = piece_ref[2 * rows :, :]
            both = piece_ref[rows : 2 * rows, :]
            top = pl.multiple_of(piece * 2 * rows, 16)
            up_ref[pl.ds(top, rows), k * width : (k + 1) * width] = both[:, : lanes // 2]
            up_ref[pl.ds(top + rows, rows), k * width : (k + 1) * width] = both[:, lanes // 2 :]


def mlp_kernel(with_long, tp, at_ref, x_ref, *refs):
    if with_long:
        xl_ref, refs = refs[0], refs[1:]
    gain_ref, atts, (o_ref, up_ref, down_ref) = refs[0], refs[1 : 1 + tp], refs[1 + tp : 4 + tp]
    outs, refs = refs[4 + tp : 4 + 2 * tp], refs[4 + 2 * tp :]
    half = x_ref.shape[1] // 2
    width = o_ref.shape[0] // tp
    x = x_ref[0].astype(F32)
    if with_long:
        xs_ref = refs[1]
        count = xl_ref.shape[1]
        xs_ref[...] = jnp.zeros_like(xs_ref)
        xs_ref[:count, :] = xl_ref[0].astype(F32)
        x = jnp.concatenate([x, xs_ref[...]], axis=0)

    def rows_of(piece):
        blocks = [piece[:half, :width], piece[:half, width:]]
        if with_long:
            blocks.append(piece[half:, :width])
        return jnp.concatenate(blocks, axis=0)

    attended = jnp.concatenate([rows_of(piece[...]) for piece in atts], axis=1)
    mid = x + dot(attended, o_ref[...])
    normed = rms_scale(mid, gain_ref[...])
    pre = dot(normed, up_ref[...])
    hidden = (pre * (0.5 + 0.5 * jnp.tanh(0.5 * pre))).astype(BF16)
    out = mid + dot(hidden, down_ref[...])
    out = out.astype(BF16)
    cols_ref = refs[0]
    for b in range(tp):
        cols = out[:, b * width : (b + 1) * width]
        cols_ref[b, :half, :] = jnp.concatenate([cols[:half], cols[half : 2 * half]], axis=1)
        if with_long:
            tail = cols[2 * half :]
            cols_ref[b, half:, :] = jnp.concatenate([tail, jnp.zeros_like(tail)], axis=1)
    for k in range(tp):
        outs[k][...] = cols_ref[at_ref[1] ^ k]


def place_kernel(tp, at_ref, *refs):
    early, late, (short_ref, long_ref) = refs[:tp], refs[tp : 2 * tp], refs[2 * tp :]
    half = early[0].shape[0]
    width = short_ref.shape[2]
    count = long_ref.shape[1]
    for k in range(tp):
        step = at_ref[1] ^ k
        for c, piece in enumerate((early[k], late[k])):
            short_ref[step, 2 * c * half : (2 * c + 1) * half, :] = piece[:half, :width]
            short_ref[step, (2 * c + 1) * half : (2 * c + 2) * half, :] = piece[:half, width:]
        long_ref[step] = late[k][half:, :width][:count]


def swap(value, axis, k):
    size = lax.axis_size(axis)
    return lax.ppermute(value, axis, [(i, i ^ k) for i in range(size)])


def whole(array):
    return pl.BlockSpec(array.shape, lambda *_: (0,) * array.ndim)


def call(kernel, at, operands, outs, specs=None, grid=(1,), scratch=(), limit=48, flops=0, name=None):
    specs = specs or {}
    return pl.pallas_call(
        kernel,
        grid_spec=pltpu.PrefetchScalarGridSpec(
            num_scalar_prefetch=1,
            grid=grid,
            in_specs=[specs.get(i, whole(a)) for i, a in enumerate(operands)],
            out_specs=[whole(o) for o in outs],
            scratch_shapes=list(scratch),
        ),
        out_shape=list(outs),
        compiler_params=pltpu.CompilerParams(vmem_limit_bytes=limit * MIB),
        cost_estimate=pl.CostEstimate(flops=flops, bytes_accessed=sum(a.size * a.dtype.itemsize for a in (*operands, *outs)), transcendentals=0),
        name=name,
    )(at, *operands)


def per_device(
    short_inputs,
    long_inputs,
    short_keys,
    short_values,
    long_keys,
    long_values,
    short_lengths,
    long_lengths,
    attn_gain,
    mlp_gain,
    query_scale,
    q_weight,
    k_weight,
    v_weight,
    o_weight,
    up_weight,
    down_weight,
):
    steps, count, model = short_inputs.shape
    long_count = long_inputs.shape[1]
    heads, head_dim = query_scale.shape
    width = heads * head_dim
    tp, seq = lax.axis_size("tp"), lax.axis_size("seq")
    slots = short_keys.shape[1]
    at = jnp.stack([lax.axis_index("seq"), lax.axis_index("tp")]).astype(jnp.int32)
    shape = jax.ShapeDtypeStruct
    attn_gain, mlp_gain = attn_gain[None], mlp_gain[None]
    short_len, long_len = short_lengths[None], long_lengths[None]

    rows, lanes = width // 4, model // 2
    (own,) = call(
        pack_kernel,
        at,
        (o_weight, up_weight, down_weight),
        (shape((3 * rows, lanes), BF16),),
        specs={
            0: pl.BlockSpec((rows, lanes), lambda _, at: ((at[0] % 8) // 2, at[0] % 2)),
            1: pl.BlockSpec((2 * rows, width), lambda _, at: (at[0] % 8, 0)),
            2: pl.BlockSpec((rows, lanes), lambda _, at: ((at[0] % 8) // 2, at[0] % 2)),
        },
        name="pack_weights",
    )
    pieces = []
    for k in range(1, tp):
        mine = swap(own, "tp", k)
        same_core = [mine] + [swap(mine, "seq", j) for j in (2, 4, 6)]
        other_core = [swap(piece, "seq", 1) for piece in same_core]
        pieces += [piece for pair in zip(same_core, other_core) for piece in pair]
    weights = call(
        functools.partial(unpack_kernel, tp),
        at,
        (o_weight, up_weight, down_weight, *pieces),
        (shape((tp * width, model), BF16), shape((model, tp * width), BF16), shape((tp * width, model), BF16)),
        name="unpack_weights",
    )

    n = steps * GROUP
    part, long_q, long_kn, long_vn = call(
        long_kernel,
        at,
        (long_inputs, long_keys, long_values, long_len, attn_gain, query_scale, q_weight, k_weight, v_weight),
        (shape((n, width + 64), F32),) + (shape((n, width), BF16),) * 3,
        scratch=(pltpu.VMEM((n, model), F32),),
        flops=2 * n * model * width * 3,
        name="long_partial",
    )
    parts = [part] + [swap(part, "seq", i) for i in range(1, seq)]

    half = count // 2
    block = 32
    tall = half // 2

    def attend(chunk, extra, extra_rows, scratch):
        first = chunk * (half // block)
        return call(
            functools.partial(short_kernel, max(0, len(extra) - 3), chunk * half),
            at,
            (short_inputs, short_keys, short_values, short_len, attn_gain, query_scale, q_weight, k_weight, v_weight, *extra),
            (shape((tall + extra_rows, 2 * width), BF16),) * steps,
            specs={
                0: pl.BlockSpec((steps, block, model), lambda i, at: (0, first + i, 0)),
                1: pl.BlockSpec((block, slots, width), lambda i, at: (first + i, 0, 0)),
                2: pl.BlockSpec((block, slots, width), lambda i, at: (first + i, 0, 0)),
            },
            grid=(half // block,),
            scratch=(pltpu.VMEM((steps, half, width), BF16), *scratch),
            flops=2 * steps * half * model * width * 3,
            name="short_attention",
        )

    early = attend(0, (), 0, ())
    early = [early[0]] + [swap(early[k], "tp", k) for k in range(1, tp)]
    late = attend(
        1,
        (*parts, long_q, long_kn, long_vn),
        GROUP,
        (pltpu.VMEM((steps, GROUP, width), BF16), pltpu.VMEM((seq, n, width + 64), F32)),
    )
    late = [late[0]] + [swap(late[k], "tp", k) for k in range(1, tp)]

    def feed_forward(chunk, pieces):
        with_long = chunk == 1
        extra = (long_inputs,) if with_long else ()
        total = half + GROUP * with_long
        specs = {0: pl.BlockSpec((1, half, model), lambda _, at: (at[1], chunk, 0))}
        if with_long:
            specs[1] = pl.BlockSpec((1, long_count, model), lambda _, at: (at[1], 0, 0))
        outs = call(
            functools.partial(mlp_kernel, with_long, tp),
            at,
            (short_inputs, *extra, mlp_gain, *pieces, *weights),
            (shape(pieces[0].shape, BF16),) * tp,
            specs=specs,
            scratch=(pltpu.VMEM((tp, *pieces[0].shape), BF16),) + ((pltpu.VMEM((GROUP, model), F32),) if with_long else ()),
            flops=2 * total * model * model * 3,
            name="feed_forward",
        )
        return [outs[0]] + [swap(outs[k], "tp", k) for k in range(1, tp)]

    early = feed_forward(0, early)
    late = feed_forward(1, late)
    return tuple(
        call(
            functools.partial(place_kernel, tp),
            at,
            (*early, *late),
            (shape((steps, count, width), BF16), shape((steps, long_count, width), BF16)),
            name="place_outputs",
        )
    )


def solution(mesh):
    return jax.shard_map(
        per_device,
        mesh=mesh,
        in_specs=(
            P(None, "seq", None),
            P(),
            P("seq", None, "tp"),
            P("seq", None, "tp"),
            P(None, "seq", "tp"),
            P(None, "seq", "tp"),
            P("seq"),
            P(),
            P(),
            P(),
            P("tp", None),
            P(None, "tp"),
            P(None, "tp"),
            P(None, "tp"),
            P("tp", None),
            P(None, "tp"),
            P("tp", None),
        ),
        out_specs=(P(None, "seq", "tp"), P(None, None, "tp")),
        check_vma=False,
    )
```

```python
import functools

import jax
import jax.numpy as jnp
from jax import lax
from jax.experimental import pallas as pl
from jax.experimental.pallas import tpu as pltpu
from jax.sharding import PartitionSpec as P

norm_eps = 1e-06
masked_fill = -1e30
GROUP = 16
F32 = jnp.float32
BF16 = jnp.bfloat16
MIB = 1024 * 1024


def rms_scale(rows, gain_row):
    mean_square = jnp.sum(rows * rows, axis=-1, keepdims=True) / rows.shape[-1]
    return (rows * lax.rsqrt(mean_square + norm_eps) * gain_row).astype(BF16)


def dot(a, b):
    return jnp.dot(a, b, preferred_element_type=F32)


def dot_t(a, b):
    return lax.dot_general(a, b, (((1,), (1,)), ((), ())), preferred_element_type=F32)


def lane_heads(rows, width, heads):
    return lax.broadcasted_iota(jnp.int32, (rows, width), 1) // (width // heads)


def stack_heads(queries, heads):
    head_of = lane_heads(*queries.shape, heads)
    return jnp.concatenate([jnp.where(head_of == h, queries, jnp.zeros_like(queries)) for h in range(heads)], axis=0)


def pick_heads(stacked, heads, width, head_dim=None):
    n = stacked.shape[0] // heads
    head_of = lax.broadcasted_iota(jnp.int32, (n, width), 1) // (head_dim or width // heads)
    picked = jnp.broadcast_to(stacked[:n], (n, width))
    for h in range(1, heads):
        picked = jnp.where(head_of == h, stacked[h * n : (h + 1) * n], picked)
    return picked


def slot_bias(lens, slots, columns):
    at = lax.broadcasted_iota(jnp.int32, (GROUP, columns), 1) - slots * lax.broadcasted_iota(jnp.int32, (GROUP, columns), 0)
    return jnp.where((at >= 0) & (at < lens), 0.0, masked_fill)


def fresh_bias(steps):
    n = steps * GROUP
    row = lax.broadcasted_iota(jnp.int32, (n, n), 0)
    col = lax.broadcasted_iota(jnp.int32, (n, n), 1)
    seen = (row % GROUP == col % GROUP) & (col // GROUP <= row // GROUP)
    return jnp.where(seen, 0.0, masked_fill)


def add_rows(scores, bias):
    reps = scores.shape[0] // bias.shape[0]
    return (scores.reshape(reps, *bias.shape) + bias[None]).reshape(scores.shape)


def pick_lens(len_row, base):
    lane = lax.broadcasted_iota(jnp.int32, (GROUP, len_row.shape[1]), 1)
    row = lax.broadcasted_iota(jnp.int32, (GROUP, len_row.shape[1]), 0)
    return jnp.sum(jnp.where(lane == base + row, len_row, 0), axis=1, keepdims=True)


def scale_lanes(scale_ref):
    return jnp.concatenate([scale_ref[h : h + 1, :] for h in range(scale_ref.shape[0])], axis=1)


def qkv_kernel(at_ref, x_ref, xl_ref, gain_ref, scale_ref, qw_ref, kw_ref, vw_ref, q_ref, kn_ref, vn_ref, ql_ref, knl_ref, vnl_ref, w_ref, rows_ref, sem):
    heads, head_dim = scale_ref.shape
    width = heads * head_dim
    short, count = x_ref.shape[1], xl_ref.shape[1]

    @pl.when(pl.program_id(0) == 0)
    def _():
        copies = [pltpu.make_async_copy(ref, w_ref.at[pl.ds(i * width, width), :], sem.at[i]) for i, ref in enumerate((qw_ref, kw_ref, vw_ref))]
        for copy in copies:
            copy.start()
        rows_ref[short:, :] = jnp.zeros((GROUP, rows_ref.shape[1]), F32)
        for copy in copies:
            copy.wait()

    rows_ref[:short, :] = x_ref[0].astype(F32)
    rows_ref[short : short + count, :] = xl_ref[0].astype(F32)
    normed = rms_scale(rows_ref[...], gain_ref[...][None])
    product = dot_t(normed, w_ref[...])
    queries = (product[:, :width] * scale_lanes(scale_ref) * head_dim**-0.5).astype(BF16)
    keys = product[:, width : 2 * width].astype(BF16)
    values = product[:, 2 * width :].astype(BF16)
    for rows, short_ref, long_ref in ((queries, q_ref, ql_ref), (keys, kn_ref, knl_ref), (values, vn_ref, vnl_ref)):
        short_ref[0] = rows[:short]
        long_ref[0] = rows[short:]


def put_sums(part_ref, row_max, weight_sum, width, heads):
    n = part_ref.shape[0]
    lane = lax.broadcasted_iota(jnp.int32, (n, part_ref.shape[1] - width), 1)
    tail = jnp.zeros(lane.shape, F32)
    for h in range(heads):
        tail = jnp.where(lane == h, row_max[h * n : (h + 1) * n], tail)
        tail = jnp.where(lane == heads + h, weight_sum[h * n : (h + 1) * n], tail)
    part_ref[:, width:] = tail


def get_column(part, first, heads):
    return jnp.concatenate([part[:, first + h : first + h + 1] for h in range(heads)], axis=0)


def long_kernel(heads, at_ref, q_ref, k_ref, v_ref, len_ref, part_ref):
    steps, _, width = q_ref.shape
    count, slots, _ = k_ref.shape
    n = steps * GROUP
    lens = jnp.minimum(pick_lens(len_ref[...][None], 0) - at_ref[0] * slots, slots)
    keys = k_ref[...].reshape(count * slots, width)
    values = v_ref[...].reshape(count * slots, width)
    bias = slot_bias(lens, slots, count * slots)
    scores = add_rows(dot_t(stack_heads(q_ref[...].reshape(n, width), heads), keys), bias)
    row_max = jnp.max(scores, axis=1, keepdims=True)
    probs = jnp.where(scores > 0.5 * masked_fill, jnp.exp(scores - row_max), 0.0)
    weight_sum = jnp.sum(probs, axis=1, keepdims=True)
    part_ref[:, :width] = pick_heads(dot(probs.astype(BF16), values), heads, width)
    put_sums(part_ref, row_max, weight_sum, width, heads)


def pair_kernel(heads, width, at_ref, mine_ref, other_ref, out_ref):
    even = at_ref[0] % 2 == 0
    mine, other = mine_ref[...], other_ref[...]
    parts = (jnp.where(even, mine, other), jnp.where(even, other, mine))
    maxes = [get_column(part, width, heads) for part in parts]
    row_max = jnp.maximum(*maxes)
    weight_sum = jnp.zeros_like(row_max)
    acc = jnp.zeros((mine.shape[0], width), F32)
    for part, part_max in zip(parts, maxes):
        factor = jnp.exp(part_max - row_max)
        weight_sum = weight_sum + factor * get_column(part, width + heads, heads)
        acc = acc + part[:, :width] * pick_heads(factor, heads, width)
    out_ref[:, :width] = acc
    put_sums(out_ref, row_max, weight_sum, width, heads)


def merge_long(my_chip, parts, held_ref, q, kn, vn, heads):
    n, width = q.shape
    for i, part in enumerate(parts):
        held_ref[my_chip ^ i] = part[...]
    scores = add_rows(dot_t(stack_heads(q, heads), kn), fresh_bias(n // GROUP))
    total_max = jnp.max(scores, axis=1, keepdims=True)
    held = [held_ref[i] for i in range(len(parts))]
    maxes = [get_column(part, width, heads) for part in held]
    for part_max in maxes:
        total_max = jnp.maximum(total_max, part_max)
    probs = jnp.exp(scores - total_max)
    denom = jnp.sum(probs, axis=1, keepdims=True)
    acc = pick_heads(dot(probs.astype(BF16), vn), heads, width)
    for part, part_max in zip(held, maxes):
        factor = jnp.exp(part_max - total_max)
        denom = denom + factor * get_column(part, width + heads, heads)
        acc = acc + part[:, :width] * pick_heads(factor, heads, width)
    return acc / pick_heads(denom, heads, width)


def short_kernel(heads, at_ref, q_ref, kn_ref, vn_ref, k_ref, v_ref, len_ref, *refs):
    att_ref = refs[-1]
    steps, block, width = q_ref.shape
    slots = k_ref.shape[1]
    few = GROUP // 2
    n = steps * few
    cached = few * slots
    i = pl.program_id(0)
    row = lax.broadcasted_iota(jnp.int32, (n, n), 0)
    col = lax.broadcasted_iota(jnp.int32, (n, n), 1)
    seen = (row % few == col % few) & (col // few <= row // few)
    late = jnp.where(seen, 0.0, masked_fill)
    slot = lax.broadcasted_iota(jnp.int32, (few, cached), 1) - slots * lax.broadcasted_iota(jnp.int32, (few, cached), 0)
    lane = lax.broadcasted_iota(jnp.int32, (few, len_ref.shape[0]), 1)
    request = lax.broadcasted_iota(jnp.int32, (few, len_ref.shape[0]), 0)
    groups = range(block // few)
    queries, keys, values, biases = [], [], [], []
    for g in groups:
        at, lo = slice(g * few, (g + 1) * few), g // 2 * GROUP
        half = g % 2 * few
        new = [ref[:, lo : lo + GROUP, :].astype(F32)[:, half : half + few, :].reshape(n, width).astype(BF16) for ref in (q_ref, kn_ref, vn_ref)]
        queries.append(stack_heads(new[0], heads))
        keys.append(jnp.concatenate([k_ref[at].reshape(cached, width), new[1]], axis=0))
        values.append(jnp.concatenate([v_ref[at].reshape(cached, width), new[2]], axis=0))
        lens = jnp.sum(jnp.where(lane == i * block + g * few + request, len_ref[...][None], 0), axis=1, keepdims=True)
        bias = jnp.where((slot >= 0) & (slot < lens), 0.0, masked_fill)
        biases.append(jnp.concatenate([jnp.concatenate([bias] * steps, axis=0), late], axis=1))
    scores = [add_rows(dot_t(queries[g], keys[g]), biases[g]) for g in groups]
    row_max = [jnp.max(scores[g], axis=1, keepdims=True) for g in groups]
    probs = [jnp.exp(scores[g] - row_max[g]) for g in groups]
    inverse = [1.0 / jnp.sum(probs[g], axis=1, keepdims=True) for g in groups]
    probs = [probs[g].astype(BF16) for g in groups]
    weighted = [dot(probs[g], values[g]) for g in groups]
    outs = [pick_heads(weighted[g] * inverse[g], heads, width) for g in groups]
    for g in groups[::2]:
        for s in range(steps):
            both = jnp.concatenate([outs[g][s * few : (s + 1) * few], outs[g + 1][s * few : (s + 1) * few]], axis=0)
            att_ref[s, g * few : (g + 2) * few, :] = both.astype(BF16)


def send_kernel(heads, at_ref, att_ref, ql_ref, knl_ref, vnl_ref, *refs):
    steps, count, width = att_ref.shape
    parts, outs, (long_ref, held_ref) = refs[: -2 - steps], refs[-2 - steps : -2], refs[-2:]
    half, n = count // 2, steps * GROUP
    longs = [ref[...].reshape(n, width) for ref in (ql_ref, knl_ref, vnl_ref)]
    merged = merge_long(at_ref[0] // 2, parts, held_ref, *longs, heads)
    for s in range(steps):
        long_ref[s] = merged[s * GROUP : (s + 1) * GROUP]
    for k in range(steps):
        rows = att_ref[at_ref[1] ^ k]
        mine = long_ref[at_ref[1] ^ k]
        outs[k][:half, :] = jnp.concatenate([rows[:half], rows[half:]], axis=1)
        outs[k][half:, :] = jnp.concatenate([mine[: GROUP // 2], mine[GROUP // 2 :]], axis=1).astype(BF16)


def pack_kernel(at_ref, o_ref, up_ref, down_ref, out_ref):
    for i, ref in enumerate((o_ref, up_ref, down_ref)):
        out_ref[i] = ref[...]


def stack_kernel(count, at_ref, *refs):
    for i in range(count):
        refs[-1][3 * i : 3 * i + 3] = refs[i][...]


def cut_kernel(cut, at_ref, x_ref, y_ref, *refs):
    refs[-2][...] = y_ref[:cut]
    refs[-1][...] = x_ref[cut:]


def mlp_kernel(tp, at_ref, x_ref, xl_ref, gain_ref, *refs):
    atts, owns, refs = refs[:tp], refs[tp : tp + 3], refs[tp + 3 :]
    pieces, outs, (cols_ref, xs_ref, w_ref, sem) = refs[: -tp - 4], refs[-tp - 4 : -4], refs[-4:]
    width, model = owns[0].shape
    rows, lanes = pieces[0].shape[1:]
    mine = at_ref[0] % 8
    copies = [pltpu.make_async_copy(ref, w_ref.at[i, pl.ds(0, width), :], sem.at[i]) for i, ref in enumerate(owns)]
    first = pieces[6].shape[0]
    for i, piece in enumerate(pieces):
        chip, start = (min(i // 2, 3), first if i // 2 == 4 else 0)
        place = mine ^ (2 * chip + i % 2)
        at = start
        while at < start + piece.shape[0]:
            unit, share = at // 3, at % 3
            size = min(3 - share, start + piece.shape[0] - at)
            row = pl.multiple_of((unit + 1) * width + (place // 2) * rows, 16)
            lane = pl.multiple_of((place % 2) * lanes, 128)
            target = w_ref.at[pl.ds(share, size), pl.ds(row, rows), pl.ds(lane, lanes)]
            copies.append(pltpu.make_async_copy(piece.at[pl.ds(at - start, size)], target, sem.at[len(copies)]))
            at += size
    for copy in copies:
        copy.start()
    half = x_ref.shape[1] // 2
    count = xl_ref.shape[1]
    xs_ref[...] = jnp.zeros_like(xs_ref)
    xs_ref[:count, :] = xl_ref[0].astype(F32)
    x = jnp.concatenate([x_ref[0].astype(F32), xs_ref[...]], axis=0)

    def rows_of(piece):
        tail = piece[half:].astype(F32)
        tail = jnp.concatenate([tail[:, :width], tail[:, width:]], axis=0).astype(BF16)
        return jnp.concatenate([piece[:half, :width], piece[:half, width:], tail], axis=0)

    attended = jnp.concatenate([rows_of(piece[...]) for piece in atts], axis=1)
    for copy in copies:
        copy.wait()
    mid = x + dot(attended, w_ref[0])
    normed = rms_scale(mid, gain_ref[...][None])
    pre = dot_t(normed, w_ref[1])
    hidden = (pre * (0.5 + 0.5 * jnp.tanh(0.5 * pre))).astype(BF16)
    out = mid + dot(hidden, w_ref[2])
    for b in range(tp):
        cols = out[:, b * width : (b + 1) * width]
        cols_ref[b, :half, :] = jnp.concatenate([cols[:half], cols[half : 2 * half]], axis=1).astype(BF16)
        tail = cols[2 * half :]
        cols_ref[b, half:, :] = jnp.concatenate([tail[: GROUP // 2], tail[GROUP // 2 :]], axis=1).astype(BF16)
    for k in range(tp):
        outs[k][...] = cols_ref[at_ref[1] ^ k]


def place_kernel(tp, at_ref, *refs):
    pieces, (short_ref, long_ref) = refs[:tp], refs[tp:]
    half, width = short_ref.shape[1] // 2, short_ref.shape[2]
    count = long_ref.shape[1]
    for k in range(tp):
        step = at_ref[1] ^ k
        short_ref[step, :half, :] = pieces[k][:half, :width]
        short_ref[step, half:, :] = pieces[k][:half, width:]
        tail = pieces[k][half:, :].astype(F32)
        long_ref[step] = jnp.concatenate([tail[:, :width], tail[:, width:]], axis=0)[:count].astype(BF16)


def swap(value, axis, k):
    size = lax.axis_size(axis)
    return lax.ppermute(value, axis, [(i, i ^ k) for i in range(size)])


def whole(array):
    return pl.BlockSpec(array.shape, lambda *_: (0,) * array.ndim)


def call(kernel, at, operands, outs, specs=None, out_specs=None, grid=(1,), scratch=(), limit=16, flops=0, moved=1024, name=None):
    specs, out_specs = specs or {}, out_specs or {}
    return pl.pallas_call(
        kernel,
        grid_spec=pltpu.PrefetchScalarGridSpec(
            num_scalar_prefetch=1,
            grid=grid,
            in_specs=[specs.get(i, whole(a)) for i, a in enumerate(operands)],
            out_specs=[out_specs.get(i, whole(o)) for i, o in enumerate(outs)],
            scratch_shapes=list(scratch),
        ),
        out_shape=list(outs),
        compiler_params=pltpu.CompilerParams(vmem_limit_bytes=limit * MIB),
        cost_estimate=pl.CostEstimate(flops=flops, bytes_accessed=moved, transcendentals=0),
        name=name,
    )(at, *operands)


def per_device(
    short_inputs,
    long_inputs,
    short_keys,
    short_values,
    long_keys,
    long_values,
    short_lengths,
    long_lengths,
    attn_gain,
    mlp_gain,
    query_scale,
    q_weight,
    k_weight,
    v_weight,
    o_weight,
    up_weight,
    down_weight,
):
    steps, count, model = short_inputs.shape
    long_count = long_inputs.shape[1]
    heads, head_dim = query_scale.shape
    width = heads * head_dim
    tp, seq = lax.axis_size("tp"), lax.axis_size("seq")
    slots = short_keys.shape[1]
    at = jnp.stack([lax.axis_index("seq"), lax.axis_index("tp")]).astype(jnp.int32)
    shape = jax.ShapeDtypeStruct
    in_hbm = pl.BlockSpec(memory_space=pltpu.HBM)
    short_len, long_len = short_lengths, long_lengths

    rows, lanes = width // 4, model // 2
    shares = (o_weight, up_weight.T, down_weight)
    eighth = pl.BlockSpec((rows, lanes), lambda _, at: ((at[0] % 8) // 2, at[0] % 2))
    (own,) = call(
        pack_kernel,
        at,
        shares,
        (shape((3, rows, lanes), BF16),),
        specs={0: eighth, 1: eighth, 2: eighth},
        limit=60,
        name="pack_weights",
    )
    units = [swap(own, "tp", k) for k in range(1, tp)]

    n = steps * GROUP
    step_rows = pl.BlockSpec((1, count, width), lambda i, at: (i, 0, 0))
    long_rows = pl.BlockSpec((1, GROUP, width), lambda i, at: (i, 0, 0))
    q, kn, vn, q_long, kn_long, vn_long = call(
        qkv_kernel,
        at,
        (short_inputs, long_inputs, attn_gain, query_scale, q_weight.T, k_weight.T, v_weight.T),
        (shape((steps, count, width), BF16),) * 3 + (shape((steps, GROUP, width), BF16),) * 3,
        specs={
            0: pl.BlockSpec((1, count, model), lambda i, at: (i, 0, 0)),
            1: pl.BlockSpec((1, long_count, model), lambda i, at: (i, 0, 0)),
            4: in_hbm,
            5: in_hbm,
            6: in_hbm,
        },
        out_specs={0: step_rows, 1: step_rows, 2: step_rows, 3: long_rows, 4: long_rows, 5: long_rows},
        grid=(steps,),
        scratch=(pltpu.VMEM((3 * width, model), BF16), pltpu.VMEM((count + GROUP, model), F32), pltpu.SemaphoreType.DMA((3,))),
        limit=60,
        name="qkv",
    )

    part_shape = shape((n, width + 64), F32)
    (part,) = call(functools.partial(long_kernel, heads), at, (q_long, long_keys, long_values, long_len), (part_shape,), name="long_partial")
    (part,) = call(functools.partial(pair_kernel, heads, width), at, (part, swap(part, "seq", 1)), (part_shape,), name="long_pair")
    parts = [part] + [swap(part, "seq", 2 * i) for i in range(1, seq // 2)]

    block = count // 2
    packed = shape((count // 2 + GROUP // 2, 2 * width), BF16)
    fresh_rows = pl.BlockSpec((steps, block, width), lambda i, at: (0, i, 0))
    cache_rows = pl.BlockSpec((block, slots, width), lambda i, at: (i, 0, 0))
    (att,) = call(
        functools.partial(short_kernel, heads),
        at,
        (q, kn, vn, short_keys, short_values, short_len, part),
        (shape((steps, count, width), BF16),),
        specs={0: fresh_rows, 1: fresh_rows, 2: fresh_rows, 3: cache_rows, 4: cache_rows, 6: in_hbm},
        out_specs={0: fresh_rows},
        grid=(count // block,),
        limit=60,
        name="short_attention",
    )
    att_sent = call(
        functools.partial(send_kernel, heads),
        at,
        (att, q_long, kn_long, vn_long, *parts),
        (packed,) * steps,
        scratch=(pltpu.VMEM((steps, GROUP, width), F32), pltpu.VMEM((seq // 2, n, width + 64), F32)),
        name="send_attended",
    )
    received = [att_sent[0]] + [swap(att_sent[k], "tp", k) for k in range(1, tp)]

    blocks = 3 * (tp - 1)
    cut = blocks // 2 + 1
    (mine,) = call(
        functools.partial(stack_kernel, tp - 1),
        at,
        (*units, att, *parts[1:]),
        (shape((blocks, rows, lanes), BF16),),
        specs={tp - 1 + i: in_hbm for i in range(len(parts))},
        name="stack_weights",
    )
    along_x, along_y = swap(mine, "seq", 2), swap(mine, "seq", 4)
    first, second = call(
        functools.partial(cut_kernel, cut),
        at,
        (along_x, along_y, *received[1:]),
        (shape((cut, rows, lanes), BF16), shape((blocks - cut, rows, lanes), BF16)),
        specs={2 + i: in_hbm for i in range(tp - 1)},
        name="cut_weights",
    )
    spread = [mine, along_x, along_y, swap(first, "seq", 2), swap(second, "seq", 4)]
    pieces = [piece for held in spread for piece in (held, swap(held, "seq", 1))]

    outs = call(
        functools.partial(mlp_kernel, tp),
        at,
        (short_inputs, long_inputs, mlp_gain, *received, *shares, *pieces),
        (packed,) * tp,
        specs={
            0: pl.BlockSpec((1, count, model), lambda _, at: (at[1], 0, 0)),
            1: pl.BlockSpec((1, long_count, model), lambda _, at: (at[1], 0, 0)),
            **{3 + tp + i: in_hbm for i in range(3 + len(pieces))},
        },
        scratch=(
            pltpu.VMEM((tp, *packed.shape), BF16),
            pltpu.VMEM((GROUP, model), F32),
            pltpu.VMEM((3, tp * width, model), BF16),
            pltpu.SemaphoreType.DMA((3 + 9 * (tp - 1),)),
        ),
        flops=2 * (count + GROUP) * model * model * 3,
        limit=36,
        name="feed_forward",
    )
    outs = [outs[0]] + [swap(outs[k], "tp", k) for k in range(1, tp)]
    return tuple(
        call(
            functools.partial(place_kernel, tp),
            at,
            outs,
            (shape((steps, count, width), BF16), shape((steps, long_count, width), BF16)),
            name="place_outputs",
        )
    )


def solution(mesh):
    return jax.shard_map(
        per_device,
        mesh=mesh,
        in_specs=(
            P(None, "seq", None),
            P(),
            P("seq", None, "tp"),
            P("seq", None, "tp"),
            P(None, "seq", "tp"),
            P(None, "seq", "tp"),
            P("seq"),
            P(),
            P(),
            P(),
            P("tp", None),
            P(None, "tp"),
            P(None, "tp"),
            P(None, "tp"),
            P("tp", None),
            P(None, "tp"),
            P("tp", None),
        ),
        out_specs=(P(None, "seq", "tp"), P(None, None, "tp")),
        check_vma=False,
    )
```

```python
import functools

import jax
import jax.numpy as jnp
from jax import lax
from jax.experimental import pallas as pl
from jax.experimental.pallas import tpu as pltpu
from jax.sharding import PartitionSpec as P

norm_eps = 1e-06
masked_fill = -1e30
GROUP = 16
F32 = jnp.float32
BF16 = jnp.bfloat16
MIB = 1024 * 1024


def rms_scale(rows, gain_row):
    mean_square = jnp.sum(rows * rows, axis=-1, keepdims=True) / rows.shape[-1]
    return (rows * lax.rsqrt(mean_square + norm_eps) * gain_row).astype(BF16)


def dot(a, b):
    return jnp.dot(a, b, preferred_element_type=F32)


def dot_t(a, b):
    return lax.dot_general(a, b, (((1,), (1,)), ((), ())), preferred_element_type=F32)


def lane_heads(rows, width, heads):
    return lax.broadcasted_iota(jnp.int32, (rows, width), 1) // (width // heads)


def stack_heads(queries, heads):
    head_of = lane_heads(*queries.shape, heads)
    return jnp.concatenate([jnp.where(head_of == h, queries, jnp.zeros_like(queries)) for h in range(heads)], axis=0)


def pick_heads(stacked, heads, width, head_dim=None):
    n = stacked.shape[0] // heads
    head_of = lax.broadcasted_iota(jnp.int32, (n, width), 1) // (head_dim or width // heads)
    picked = jnp.broadcast_to(stacked[:n], (n, width))
    for h in range(1, heads):
        picked = jnp.where(head_of == h, stacked[h * n : (h + 1) * n], picked)
    return picked


def slot_bias(lens, slots, columns):
    at = lax.broadcasted_iota(jnp.int32, (GROUP, columns), 1) - slots * lax.broadcasted_iota(jnp.int32, (GROUP, columns), 0)
    return jnp.where((at >= 0) & (at < lens), 0.0, masked_fill)


def fresh_bias(steps):
    n = steps * GROUP
    row = lax.broadcasted_iota(jnp.int32, (n, n), 0)
    col = lax.broadcasted_iota(jnp.int32, (n, n), 1)
    seen = (row % GROUP == col % GROUP) & (col // GROUP <= row // GROUP)
    return jnp.where(seen, 0.0, masked_fill)


def add_rows(scores, bias):
    reps = scores.shape[0] // bias.shape[0]
    return (scores.reshape(reps, *bias.shape) + bias[None]).reshape(scores.shape)


def pick_lens(len_row, base):
    lane = lax.broadcasted_iota(jnp.int32, (GROUP, len_row.shape[1]), 1)
    row = lax.broadcasted_iota(jnp.int32, (GROUP, len_row.shape[1]), 0)
    return jnp.sum(jnp.where(lane == base + row, len_row, 0), axis=1, keepdims=True)


def step_rows_of(rows, step):
    at = lax.broadcasted_iota(jnp.int32, rows.shape, 1)
    return jnp.sum(jnp.where(at == step, rows.astype(F32), 0.0), axis=1)


def scale_lanes(scale_ref):
    return jnp.concatenate([scale_ref[h : h + 1, :] for h in range(scale_ref.shape[0])], axis=1)


def qkv_kernel(at_ref, x_ref, xl_ref, gain_ref, scale_ref, qw_ref, kw_ref, vw_ref, q_ref, kn_ref, vn_ref, ql_ref, knl_ref, vnl_ref, w_ref, rows_ref, sem):
    heads, head_dim = scale_ref.shape
    width = heads * head_dim
    short, count = x_ref.shape[1], xl_ref.shape[0]

    @pl.when(pl.program_id(0) == 0)
    def _():
        copies = [pltpu.make_async_copy(ref, w_ref.at[pl.ds(i * width, width), :], sem.at[i]) for i, ref in enumerate((qw_ref, kw_ref, vw_ref))]
        for copy in copies:
            copy.start()
        rows_ref[short:, :] = jnp.zeros((GROUP, rows_ref.shape[1]), F32)
        for copy in copies:
            copy.wait()

    rows_ref[:short, :] = x_ref[0].astype(F32)
    rows_ref[short : short + count, :] = step_rows_of(xl_ref[...], pl.program_id(0))
    normed = rms_scale(rows_ref[...], gain_ref[...][None])
    product = dot_t(normed, w_ref[...])
    queries = (product[:, :width] * scale_lanes(scale_ref) * head_dim**-0.5).astype(BF16)
    keys = product[:, width : 2 * width].astype(BF16)
    values = product[:, 2 * width :].astype(BF16)
    for rows, short_ref, long_ref in ((queries, q_ref, ql_ref), (keys, kn_ref, knl_ref), (values, vn_ref, vnl_ref)):
        short_ref[0] = rows[:short]
        long_ref[0] = rows[short:]


def put_sums(part_ref, row_max, weight_sum, width, heads):
    n = part_ref.shape[0]
    lane = lax.broadcasted_iota(jnp.int32, (n, part_ref.shape[1] - width), 1)
    tail = jnp.zeros(lane.shape, F32)
    for h in range(heads):
        tail = jnp.where(lane == h, row_max[h * n : (h + 1) * n], tail)
        tail = jnp.where(lane == heads + h, weight_sum[h * n : (h + 1) * n], tail)
    part_ref[:, width:] = tail


def get_column(part, first, heads):
    return jnp.concatenate([part[:, first + h : first + h + 1] for h in range(heads)], axis=0)


def long_kernel(heads, at_ref, q_ref, k_ref, v_ref, len_ref, part_ref):
    steps, _, width = q_ref.shape
    count, slots, _ = k_ref.shape
    n = steps * GROUP
    lens = jnp.minimum(pick_lens(len_ref[...][None], 0) - at_ref[0] * slots, slots)
    keys = k_ref[...].reshape(count * slots, width)
    values = v_ref[...].reshape(count * slots, width)
    bias = slot_bias(lens, slots, count * slots)
    scores = add_rows(dot_t(stack_heads(q_ref[...].reshape(n, width), heads), keys), bias)
    row_max = jnp.max(scores, axis=1, keepdims=True)
    probs = jnp.where(scores > 0.5 * masked_fill, jnp.exp(scores - row_max), 0.0)
    weight_sum = jnp.sum(probs, axis=1, keepdims=True)
    part_ref[:, :width] = pick_heads(dot(probs.astype(BF16), values), heads, width)
    put_sums(part_ref, row_max, weight_sum, width, heads)


def pair_kernel(heads, width, at_ref, mine_ref, other_ref, after_ref, out_ref):
    even = at_ref[0] % 2 == 0
    mine, other = mine_ref[...], other_ref[...]
    parts = (jnp.where(even, mine, other), jnp.where(even, other, mine))
    maxes = [get_column(part, width, heads) for part in parts]
    row_max = jnp.maximum(*maxes)
    weight_sum = jnp.zeros_like(row_max)
    acc = jnp.zeros((mine.shape[0], width), F32)
    for part, part_max in zip(parts, maxes):
        factor = jnp.exp(part_max - row_max)
        weight_sum = weight_sum + factor * get_column(part, width + heads, heads)
        acc = acc + part[:, :width] * pick_heads(factor, heads, width)
    out_ref[:, :width] = acc
    put_sums(out_ref, row_max, weight_sum, width, heads)


def merge_long(my_chip, parts, held_ref, q, kn, vn, heads):
    n, width = q.shape
    for i, part in enumerate(parts):
        held_ref[my_chip ^ i] = part[...]
    scores = add_rows(dot_t(stack_heads(q, heads), kn), fresh_bias(n // GROUP))
    total_max = jnp.max(scores, axis=1, keepdims=True)
    held = [held_ref[i] for i in range(len(parts))]
    maxes = [get_column(part, width, heads) for part in held]
    for part_max in maxes:
        total_max = jnp.maximum(total_max, part_max)
    probs = jnp.exp(scores - total_max)
    denom = jnp.sum(probs, axis=1, keepdims=True)
    acc = pick_heads(dot(probs.astype(BF16), vn), heads, width)
    for part, part_max in zip(held, maxes):
        factor = jnp.exp(part_max - total_max)
        denom = denom + factor * get_column(part, width + heads, heads)
        acc = acc + part[:, :width] * pick_heads(factor, heads, width)
    return acc / pick_heads(denom, heads, width)


def short_kernel(heads, at_ref, q_ref, kn_ref, vn_ref, k_ref, v_ref, len_ref, *refs):
    att_ref = refs[-1]
    steps, block, width = q_ref.shape
    slots = k_ref.shape[1]
    few = GROUP // 2
    n = steps * few
    cached = few * slots
    i = pl.program_id(0)
    row = lax.broadcasted_iota(jnp.int32, (n, n), 0)
    col = lax.broadcasted_iota(jnp.int32, (n, n), 1)
    seen = (row % few == col % few) & (col // few <= row // few)
    late = jnp.where(seen, 0.0, masked_fill)
    slot = lax.broadcasted_iota(jnp.int32, (few, cached), 1) - slots * lax.broadcasted_iota(jnp.int32, (few, cached), 0)
    lane = lax.broadcasted_iota(jnp.int32, (few, len_ref.shape[0]), 1)
    request = lax.broadcasted_iota(jnp.int32, (few, len_ref.shape[0]), 0)
    groups = range(block // few)
    queries, keys, values, biases = [], [], [], []
    for g in groups:
        at, lo = slice(g * few, (g + 1) * few), g // 2 * GROUP
        half = g % 2 * few
        new = [ref[:, lo : lo + GROUP, :].astype(F32)[:, half : half + few, :].reshape(n, width).astype(BF16) for ref in (q_ref, kn_ref, vn_ref)]
        queries.append(stack_heads(new[0], heads))
        keys.append(jnp.concatenate([k_ref[at].reshape(cached, width), new[1]], axis=0))
        values.append(jnp.concatenate([v_ref[at].reshape(cached, width), new[2]], axis=0))
        lens = jnp.sum(jnp.where(lane == i * block + g * few + request, len_ref[...][None], 0), axis=1, keepdims=True)
        bias = jnp.where((slot >= 0) & (slot < lens), 0.0, masked_fill)
        biases.append(jnp.concatenate([jnp.concatenate([bias] * steps, axis=0), late], axis=1))
    scores = [add_rows(dot_t(queries[g], keys[g]), biases[g]) for g in groups]
    row_max = [jnp.max(scores[g], axis=1, keepdims=True) for g in groups]
    probs = [jnp.exp(scores[g] - row_max[g]) for g in groups]
    inverse = [1.0 / jnp.sum(probs[g], axis=1, keepdims=True) for g in groups]
    probs = [probs[g].astype(BF16) for g in groups]
    weighted = [dot(probs[g], values[g]) for g in groups]
    outs = [pick_heads(weighted[g] * inverse[g], heads, width) for g in groups]
    for g in groups[::2]:
        for s in range(steps):
            both = jnp.concatenate([outs[g][s * few : (s + 1) * few], outs[g + 1][s * few : (s + 1) * few]], axis=0)
            att_ref[s, g * few : (g + 2) * few, :] = both.astype(BF16)


def send_kernel(heads, at_ref, att_ref, ql_ref, knl_ref, vnl_ref, *refs):
    steps, count, width = att_ref.shape
    parts, outs, (long_ref, held_ref) = refs[: -2 - steps], refs[-2 - steps : -2], refs[-2:]
    half, n = count // 2, steps * GROUP
    longs = [ref[...].reshape(n, width) for ref in (ql_ref, knl_ref, vnl_ref)]
    merged = merge_long(at_ref[0] // 2, parts, held_ref, *longs, heads)
    for s in range(steps):
        long_ref[s] = merged[s * GROUP : (s + 1) * GROUP]
    for k in range(steps):
        rows = att_ref[at_ref[1] ^ k]
        mine = long_ref[at_ref[1] ^ k]
        outs[k][:half, :] = jnp.concatenate([rows[:half], rows[half:]], axis=1)
        outs[k][half:, :] = jnp.concatenate([mine[: GROUP // 2], mine[GROUP // 2 :]], axis=1).astype(BF16)


def pack_kernel(at_ref, o_ref, up_ref, down_ref, out_ref):
    for i, ref in enumerate((o_ref, up_ref, down_ref)):
        out_ref[i] = ref[...]


def stack_kernel(count, at_ref, *refs):
    for i in range(count):
        refs[-1][3 * i : 3 * i + 3] = refs[i][...]


def cut_kernel(cut, at_ref, x_ref, y_ref, *refs):
    refs[-2][...] = y_ref[:cut]
    refs[-1][...] = x_ref[cut:]


def mlp_kernel(tp, at_ref, x_ref, xl_ref, gain_ref, *refs):
    atts, owns, refs = refs[:tp], refs[tp : tp + 3], refs[tp + 3 :]
    pieces, outs, (cols_ref, xs_ref, w_ref, sem) = refs[: -tp - 4], refs[-tp - 4 : -4], refs[-4:]
    width, model = owns[0].shape
    rows, lanes = pieces[0].shape[1:]
    mine = at_ref[0] % 8
    copies = [pltpu.make_async_copy(ref, w_ref.at[i, pl.ds(0, width), :], sem.at[i]) for i, ref in enumerate(owns)]
    first = pieces[6].shape[0]
    for i, piece in enumerate(pieces):
        chip, start = (min(i // 2, 3), first if i // 2 == 4 else 0)
        place = mine ^ (2 * chip + i % 2)
        at = start
        while at < start + piece.shape[0]:
            unit, share = at // 3, at % 3
            size = min(3 - share, start + piece.shape[0] - at)
            row = pl.multiple_of((unit + 1) * width + (place // 2) * rows, 16)
            lane = pl.multiple_of((place % 2) * lanes, 128)
            target = w_ref.at[pl.ds(share, size), pl.ds(row, rows), pl.ds(lane, lanes)]
            copies.append(pltpu.make_async_copy(piece.at[pl.ds(at - start, size)], target, sem.at[len(copies)]))
            at += size
    for copy in copies:
        copy.start()
    half = x_ref.shape[1] // 2
    count = xl_ref.shape[0]
    xs_ref[...] = jnp.zeros_like(xs_ref)
    xs_ref[:count, :] = step_rows_of(xl_ref[...], at_ref[1])
    x = jnp.concatenate([x_ref[0].astype(F32), xs_ref[...]], axis=0)

    def rows_of(piece):
        tail = piece[half:].astype(F32)
        tail = jnp.concatenate([tail[:, :width], tail[:, width:]], axis=0).astype(BF16)
        return jnp.concatenate([piece[:half, :width], piece[:half, width:], tail], axis=0)

    attended = jnp.concatenate([rows_of(piece[...]) for piece in atts], axis=1)
    for copy in copies:
        copy.wait()
    mid = x + dot(attended, w_ref[0])
    normed = rms_scale(mid, gain_ref[...][None])
    pre = dot_t(normed, w_ref[1])
    hidden = (pre * (0.5 + 0.5 * jnp.tanh(0.5 * pre))).astype(BF16)
    out = mid + dot(hidden, w_ref[2])
    for b in range(tp):
        cols = out[:, b * width : (b + 1) * width]
        cols_ref[b, :half, :] = jnp.concatenate([cols[:half], cols[half : 2 * half]], axis=1).astype(BF16)
        tail = cols[2 * half :]
        cols_ref[b, half:, :] = jnp.concatenate([tail[: GROUP // 2], tail[GROUP // 2 :]], axis=1).astype(BF16)
    for k in range(tp):
        outs[k][...] = cols_ref[at_ref[1] ^ k]


def place_kernel(tp, at_ref, *refs):
    pieces, (short_ref, long_ref) = refs[:tp], refs[tp:]
    half, width = short_ref.shape[1] // 2, short_ref.shape[2]
    count = long_ref.shape[0]
    longs = jnp.zeros(long_ref.shape, F32)
    at = lax.broadcasted_iota(jnp.int32, longs.shape, 1)
    for k in range(tp):
        step = at_ref[1] ^ k
        short_ref[step, :half, :] = pieces[k][:half, :width]
        short_ref[step, half:, :] = pieces[k][:half, width:]
        tail = pieces[k][half:, :].astype(F32)
        tail = jnp.concatenate([tail[:, :width], tail[:, width:]], axis=0)[:count]
        longs = jnp.where(at == step, tail[:, None, :], longs)
    long_ref[...] = longs.astype(BF16)


def swap(value, axis, k):
    size = lax.axis_size(axis)
    return lax.ppermute(value, axis, [(i, i ^ k) for i in range(size)])


def whole(array):
    return pl.BlockSpec(array.shape, lambda *_: (0,) * array.ndim)


def call(kernel, at, operands, outs, specs=None, out_specs=None, grid=(1,), scratch=(), limit=16, flops=0, moved=1024, name=None):
    specs, out_specs = specs or {}, out_specs or {}
    return pl.pallas_call(
        kernel,
        grid_spec=pltpu.PrefetchScalarGridSpec(
            num_scalar_prefetch=1,
            grid=grid,
            in_specs=[specs.get(i, whole(a)) for i, a in enumerate(operands)],
            out_specs=[out_specs.get(i, whole(o)) for i, o in enumerate(outs)],
            scratch_shapes=list(scratch),
        ),
        out_shape=list(outs),
        compiler_params=pltpu.CompilerParams(vmem_limit_bytes=limit * MIB),
        cost_estimate=pl.CostEstimate(flops=flops, bytes_accessed=moved, transcendentals=0),
        name=name,
    )(at, *operands)


def per_device(
    short_inputs,
    long_inputs,
    short_keys,
    short_values,
    long_keys,
    long_values,
    short_lengths,
    long_lengths,
    attn_gain,
    mlp_gain,
    query_scale,
    q_weight,
    k_weight,
    v_weight,
    o_weight,
    up_weight,
    down_weight,
):
    steps, count, model = short_inputs.shape
    long_count = long_inputs.shape[1]
    heads, head_dim = query_scale.shape
    width = heads * head_dim
    tp, seq = lax.axis_size("tp"), lax.axis_size("seq")
    slots = short_keys.shape[1]
    at = jnp.stack([lax.axis_index("seq"), lax.axis_index("tp")]).astype(jnp.int32)
    shape = jax.ShapeDtypeStruct
    in_hbm = pl.BlockSpec(memory_space=pltpu.HBM)
    short_len, long_len = short_lengths, long_lengths
    long_rows_in = jnp.swapaxes(long_inputs, 0, 1)

    rows, lanes = width // 4, model // 2
    shares = (o_weight, up_weight.T, down_weight)
    eighth = pl.BlockSpec((rows, lanes), lambda _, at: ((at[0] % 8) // 2, at[0] % 2))
    (own,) = call(
        pack_kernel,
        at,
        shares,
        (shape((3, rows, lanes), BF16),),
        specs={0: eighth, 1: eighth, 2: eighth},
        limit=60,
        name="pack_weights",
    )
    units = [swap(own, "tp", k) for k in range(1, tp)]

    n = steps * GROUP
    step_rows = pl.BlockSpec((1, count, width), lambda i, at: (i, 0, 0))
    long_rows = pl.BlockSpec((1, GROUP, width), lambda i, at: (i, 0, 0))
    q, kn, vn, q_long, kn_long, vn_long = call(
        qkv_kernel,
        at,
        (short_inputs, long_rows_in, attn_gain, query_scale, q_weight.T, k_weight.T, v_weight.T),
        (shape((steps, count, width), BF16),) * 3 + (shape((steps, GROUP, width), BF16),) * 3,
        specs={
            0: pl.BlockSpec((1, count, model), lambda i, at: (i, 0, 0)),
            4: in_hbm,
            5: in_hbm,
            6: in_hbm,
        },
        out_specs={0: step_rows, 1: step_rows, 2: step_rows, 3: long_rows, 4: long_rows, 5: long_rows},
        grid=(steps,),
        scratch=(pltpu.VMEM((3 * width, model), BF16), pltpu.VMEM((count + GROUP, model), F32), pltpu.SemaphoreType.DMA((3,))),
        limit=60,
        name="qkv",
    )

    part_shape = shape((n, width + 64), F32)
    (part,) = call(functools.partial(long_kernel, heads), at, (q_long, long_keys, long_values, long_len), (part_shape,), name="long_partial")
    (part,) = call(functools.partial(pair_kernel, heads, width), at, (part, swap(part, "seq", 1), units[0]), (part_shape,), specs={2: in_hbm}, name="long_pair")
    parts = [part] + [swap(part, "seq", 2 * i) for i in range(1, seq // 2)]

    block = count // 2
    packed = shape((count // 2 + GROUP // 2, 2 * width), BF16)
    fresh_rows = pl.BlockSpec((steps, block, width), lambda i, at: (0, i, 0))
    cache_rows = pl.BlockSpec((block, slots, width), lambda i, at: (i, 0, 0))
    (att,) = call(
        functools.partial(short_kernel, heads),
        at,
        (q, kn, vn, short_keys, short_values, short_len, part),
        (shape((steps, count, width), BF16),),
        specs={0: fresh_rows, 1: fresh_rows, 2: fresh_rows, 3: cache_rows, 4: cache_rows, 6: in_hbm},
        out_specs={0: fresh_rows},
        grid=(count // block,),
        limit=50,
        name="short_attention",
    )
    att_sent = call(
        functools.partial(send_kernel, heads),
        at,
        (att, q_long, kn_long, vn_long, *parts),
        (packed,) * steps,
        scratch=(pltpu.VMEM((steps, GROUP, width), F32), pltpu.VMEM((seq // 2, n, width + 64), F32)),
        name="send_attended",
    )
    received = [att_sent[0]] + [swap(att_sent[k], "tp", k) for k in range(1, tp)]

    blocks = 3 * (tp - 1)
    cut = blocks // 2 + 1
    (mine,) = call(
        functools.partial(stack_kernel, tp - 1),
        at,
        (*units, att, *parts[1:]),
        (shape((blocks, rows, lanes), BF16),),
        specs={tp - 1 + i: in_hbm for i in range(len(parts))},
        name="stack_weights",
    )
    along_x, along_y = swap(mine, "seq", 2), swap(mine, "seq", 4)
    first, second = call(
        functools.partial(cut_kernel, cut),
        at,
        (along_x, along_y, *received[1:]),
        (shape((cut, rows, lanes), BF16), shape((blocks - cut, rows, lanes), BF16)),
        specs={2 + i: in_hbm for i in range(tp - 1)},
        name="cut_weights",
    )
    spread = [mine, along_x, along_y, swap(first, "seq", 2), swap(second, "seq", 4)]
    pieces = [piece for held in spread for piece in (held, swap(held, "seq", 1))]

    outs = call(
        functools.partial(mlp_kernel, tp),
        at,
        (short_inputs, long_rows_in, mlp_gain, *received, *shares, *pieces),
        (packed,) * tp,
        specs={
            0: pl.BlockSpec((1, count, model), lambda _, at: (at[1], 0, 0)),
            **{3 + tp + i: in_hbm for i in range(3 + len(pieces))},
        },
        scratch=(
            pltpu.VMEM((tp, *packed.shape), BF16),
            pltpu.VMEM((GROUP, model), F32),
            pltpu.VMEM((3, tp * width, model), BF16),
            pltpu.SemaphoreType.DMA((3 + 9 * (tp - 1),)),
        ),
        flops=2 * (count + GROUP) * model * model * 3,
        limit=36,
        name="feed_forward",
    )
    outs = [outs[0]] + [swap(outs[k], "tp", k) for k in range(1, tp)]
    short_out, long_out = call(
        functools.partial(place_kernel, tp),
        at,
        outs,
        (shape((steps, count, width), BF16), shape((long_count, steps, width), BF16)),
        name="place_outputs",
    )
    return short_out, jnp.swapaxes(long_out, 0, 1)


def solution(mesh):
    return jax.shard_map(
        per_device,
        mesh=mesh,
        in_specs=(
            P(None, "seq", None),
            P(),
            P("seq", None, "tp"),
            P("seq", None, "tp"),
            P(None, "seq", "tp"),
            P(None, "seq", "tp"),
            P("seq"),
            P(),
            P(),
            P(),
            P("tp", None),
            P(None, "tp"),
            P(None, "tp"),
            P(None, "tp"),
            P("tp", None),
            P(None, "tp"),
            P("tp", None),
        ),
        out_specs=(P(None, "seq", "tp"), P(None, None, "tp")),
        check_vma=False,
    )
```

```python
import functools

import jax
import jax.numpy as jnp
from jax import lax
from jax.experimental import pallas as pl
from jax.experimental.pallas import tpu as pltpu
from jax.sharding import PartitionSpec as P

norm_eps = 1e-06
masked_fill = -1e30
GROUP = 16
F32 = jnp.float32
BF16 = jnp.bfloat16
MIB = 1024 * 1024


def rms_scale(rows, gain_row):
    mean_square = jnp.sum(rows * rows, axis=-1, keepdims=True) / rows.shape[-1]
    return (rows * lax.rsqrt(mean_square + norm_eps) * gain_row).astype(BF16)


def dot(a, b):
    return jnp.dot(a, b, preferred_element_type=F32)


def dot_t(a, b):
    return lax.dot_general(a, b, (((1,), (1,)), ((), ())), preferred_element_type=F32)


def lane_heads(rows, width, heads):
    return lax.broadcasted_iota(jnp.int32, (rows, width), 1) // (width // heads)


def stack_heads(queries, heads):
    head_of = lane_heads(*queries.shape, heads)
    return jnp.concatenate([jnp.where(head_of == h, queries, jnp.zeros_like(queries)) for h in range(heads)], axis=0)


def pick_heads(stacked, heads, width, head_dim=None):
    n = stacked.shape[0] // heads
    head_of = lax.broadcasted_iota(jnp.int32, (n, width), 1) // (head_dim or width // heads)
    picked = jnp.broadcast_to(stacked[:n], (n, width))
    for h in range(1, heads):
        picked = jnp.where(head_of == h, stacked[h * n : (h + 1) * n], picked)
    return picked


def slot_bias(lens, slots, columns):
    at = lax.broadcasted_iota(jnp.int32, (GROUP, columns), 1) - slots * lax.broadcasted_iota(jnp.int32, (GROUP, columns), 0)
    return jnp.where((at >= 0) & (at < lens), 0.0, masked_fill)


def fresh_bias(steps):
    n = steps * GROUP
    row = lax.broadcasted_iota(jnp.int32, (n, n), 0)
    col = lax.broadcasted_iota(jnp.int32, (n, n), 1)
    seen = (row % GROUP == col % GROUP) & (col // GROUP <= row // GROUP)
    return jnp.where(seen, 0.0, masked_fill)


def add_rows(scores, bias):
    reps = scores.shape[0] // bias.shape[0]
    return (scores.reshape(reps, *bias.shape) + bias[None]).reshape(scores.shape)


def pick_lens(len_row, base):
    lane = lax.broadcasted_iota(jnp.int32, (GROUP, len_row.shape[1]), 1)
    row = lax.broadcasted_iota(jnp.int32, (GROUP, len_row.shape[1]), 0)
    return jnp.sum(jnp.where(lane == base + row, len_row, 0), axis=1, keepdims=True)


def step_rows_of(rows, step):
    at = lax.broadcasted_iota(jnp.int32, rows.shape, 1)
    return jnp.sum(jnp.where(at == step, rows.astype(F32), 0.0), axis=1)


def scale_lanes(scale_ref):
    return jnp.concatenate([scale_ref[h : h + 1, :] for h in range(scale_ref.shape[0])], axis=1)


def qkv_kernel(at_ref, x_ref, xl_ref, gain_ref, scale_ref, qw_ref, kw_ref, vw_ref, q_ref, kn_ref, vn_ref, ql_ref, knl_ref, vnl_ref, w_ref, rows_ref, long_ref, sem):
    heads, head_dim = scale_ref.shape
    width = heads * head_dim
    short, count = x_ref.shape[1], xl_ref.shape[0]

    @pl.when(pl.program_id(0) == 0)
    def _():
        copies = [pltpu.make_async_copy(ref, w_ref.at[pl.ds(i * width, width), :], sem.at[i]) for i, ref in enumerate((qw_ref, kw_ref, vw_ref))]
        for copy in copies:
            copy.start()
        long_ref[...] = jnp.zeros_like(long_ref)
        for step in range(xl_ref.shape[1]):
            long_ref[step, :count, :] = xl_ref[:, step, :].astype(F32)
        for copy in copies:
            copy.wait()

    rows_ref[:short, :] = x_ref[0].astype(F32)
    rows_ref[short:, :] = long_ref[pl.program_id(0)]
    normed = rms_scale(rows_ref[...], gain_ref[...][None])
    product = dot_t(normed, w_ref[...])
    queries = (product[:, :width] * scale_lanes(scale_ref) * head_dim**-0.5).astype(BF16)
    keys = product[:, width : 2 * width].astype(BF16)
    values = product[:, 2 * width :].astype(BF16)
    for rows, short_ref, long_ref in ((queries, q_ref, ql_ref), (keys, kn_ref, knl_ref), (values, vn_ref, vnl_ref)):
        short_ref[0] = rows[:short]
        long_ref[0] = rows[short:]


def put_sums(part_ref, row_max, weight_sum, width, heads):
    n = part_ref.shape[0]
    lane = lax.broadcasted_iota(jnp.int32, (n, part_ref.shape[1] - width), 1)
    tail = jnp.zeros(lane.shape, F32)
    for h in range(heads):
        tail = jnp.where(lane == h, row_max[h * n : (h + 1) * n], tail)
        tail = jnp.where(lane == heads + h, weight_sum[h * n : (h + 1) * n], tail)
    part_ref[:, width:] = tail


def get_column(part, first, heads):
    return jnp.concatenate([part[:, first + h : first + h + 1] for h in range(heads)], axis=0)


def long_kernel(heads, at_ref, q_ref, k_ref, v_ref, len_ref, part_ref):
    steps, _, width = q_ref.shape
    count, slots, _ = k_ref.shape
    n = steps * GROUP
    lens = jnp.minimum(pick_lens(len_ref[...][None], 0) - at_ref[0] * slots, slots)
    keys = k_ref[...].reshape(count * slots, width)
    values = v_ref[...].reshape(count * slots, width)
    bias = slot_bias(lens, slots, count * slots)
    scores = add_rows(dot_t(stack_heads(q_ref[...].reshape(n, width), heads), keys), bias)
    row_max = jnp.max(scores, axis=1, keepdims=True)
    probs = jnp.where(scores > 0.5 * masked_fill, jnp.exp(scores - row_max), 0.0)
    weight_sum = jnp.sum(probs, axis=1, keepdims=True)
    part_ref[:, :width] = pick_heads(dot(probs.astype(BF16), values), heads, width)
    put_sums(part_ref, row_max, weight_sum, width, heads)


def pair_kernel(heads, width, at_ref, mine_ref, other_ref, after_ref, out_ref):
    even = at_ref[0] % 2 == 0
    mine, other = mine_ref[...], other_ref[...]
    parts = (jnp.where(even, mine, other), jnp.where(even, other, mine))
    maxes = [get_column(part, width, heads) for part in parts]
    row_max = jnp.maximum(*maxes)
    weight_sum = jnp.zeros_like(row_max)
    acc = jnp.zeros((mine.shape[0], width), F32)
    for part, part_max in zip(parts, maxes):
        factor = jnp.exp(part_max - row_max)
        weight_sum = weight_sum + factor * get_column(part, width + heads, heads)
        acc = acc + part[:, :width] * pick_heads(factor, heads, width)
    out_ref[:, :width] = acc
    put_sums(out_ref, row_max, weight_sum, width, heads)


def merge_long(my_chip, parts, held_ref, q, kn, vn, heads):
    n, width = q.shape
    for i, part in enumerate(parts):
        held_ref[my_chip ^ i] = part[...]
    scores = add_rows(dot_t(stack_heads(q, heads), kn), fresh_bias(n // GROUP))
    total_max = jnp.max(scores, axis=1, keepdims=True)
    held = [held_ref[i] for i in range(len(parts))]
    maxes = [get_column(part, width, heads) for part in held]
    for part_max in maxes:
        total_max = jnp.maximum(total_max, part_max)
    probs = jnp.exp(scores - total_max)
    denom = jnp.sum(probs, axis=1, keepdims=True)
    acc = pick_heads(dot(probs.astype(BF16), vn), heads, width)
    for part, part_max in zip(held, maxes):
        factor = jnp.exp(part_max - total_max)
        denom = denom + factor * get_column(part, width + heads, heads)
        acc = acc + part[:, :width] * pick_heads(factor, heads, width)
    return acc / pick_heads(denom, heads, width)


def short_kernel(heads, at_ref, q_ref, kn_ref, vn_ref, k_ref, v_ref, len_ref, *refs):
    att_ref = refs[-1]
    steps, block, width = q_ref.shape
    slots = k_ref.shape[1]
    few = GROUP // 2
    n = steps * few
    cached = few * slots
    i = pl.program_id(0)
    row = lax.broadcasted_iota(jnp.int32, (n, n), 0)
    col = lax.broadcasted_iota(jnp.int32, (n, n), 1)
    seen = (row % few == col % few) & (col // few <= row // few)
    late = jnp.where(seen, 0.0, masked_fill)
    slot = lax.broadcasted_iota(jnp.int32, (few, cached), 1) - slots * lax.broadcasted_iota(jnp.int32, (few, cached), 0)
    lane = lax.broadcasted_iota(jnp.int32, (few, len_ref.shape[0]), 1)
    request = lax.broadcasted_iota(jnp.int32, (few, len_ref.shape[0]), 0)
    groups = range(block // few)
    queries, keys, values, biases = [], [], [], []
    for g in groups:
        at, lo = slice(g * few, (g + 1) * few), g // 2 * GROUP
        half = g % 2 * few
        new = [ref[:, lo : lo + GROUP, :].astype(F32)[:, half : half + few, :].reshape(n, width).astype(BF16) for ref in (q_ref, kn_ref, vn_ref)]
        queries.append(stack_heads(new[0], heads))
        keys.append(jnp.concatenate([k_ref[at].reshape(cached, width), new[1]], axis=0))
        values.append(jnp.concatenate([v_ref[at].reshape(cached, width), new[2]], axis=0))
        lens = jnp.sum(jnp.where(lane == i * block + g * few + request, len_ref[...][None], 0), axis=1, keepdims=True)
        bias = jnp.where((slot >= 0) & (slot < lens), 0.0, masked_fill)
        biases.append(jnp.concatenate([jnp.concatenate([bias] * steps, axis=0), late], axis=1))
    scores = [add_rows(dot_t(queries[g], keys[g]), biases[g]) for g in groups]
    row_max = [jnp.max(scores[g], axis=1, keepdims=True) for g in groups]
    probs = [jnp.exp(scores[g] - row_max[g]) for g in groups]
    inverse = [1.0 / jnp.sum(probs[g], axis=1, keepdims=True) for g in groups]
    probs = [probs[g].astype(BF16) for g in groups]
    weighted = [dot(probs[g], values[g]) for g in groups]
    outs = [pick_heads(weighted[g] * inverse[g], heads, width) for g in groups]
    for g in groups[::2]:
        for s in range(steps):
            both = jnp.concatenate([outs[g][s * few : (s + 1) * few], outs[g + 1][s * few : (s + 1) * few]], axis=0)
            att_ref[s, g * few : (g + 2) * few, :] = both.astype(BF16)


def send_kernel(heads, at_ref, att_ref, ql_ref, knl_ref, vnl_ref, *refs):
    steps, count, width = att_ref.shape
    parts, outs, (long_ref, held_ref) = refs[: -2 - steps], refs[-2 - steps : -2], refs[-2:]
    half, n = count // 2, steps * GROUP
    longs = [ref[...].reshape(n, width) for ref in (ql_ref, knl_ref, vnl_ref)]
    merged = merge_long(at_ref[0] // 2, parts, held_ref, *longs, heads)
    for s in range(steps):
        long_ref[s] = merged[s * GROUP : (s + 1) * GROUP]
    for k in range(steps):
        rows = att_ref[at_ref[1] ^ k]
        mine = long_ref[at_ref[1] ^ k]
        outs[k][:half, :] = jnp.concatenate([rows[:half], rows[half:]], axis=1)
        outs[k][half:, :] = jnp.concatenate([mine[: GROUP // 2], mine[GROUP // 2 :]], axis=1).astype(BF16)


def pack_kernel(at_ref, o_ref, up_ref, down_ref, out_ref):
    for i, ref in enumerate((o_ref, up_ref, down_ref)):
        out_ref[i] = ref[...]


def stack_kernel(count, at_ref, *refs):
    for i in range(count):
        refs[-1][3 * i : 3 * i + 3] = refs[i][...]


def cut_kernel(cut, at_ref, x_ref, y_ref, *refs):
    refs[-2][...] = y_ref[:cut]
    refs[-1][...] = x_ref[cut:]


def mlp_kernel(tp, at_ref, x_ref, xl_ref, gain_ref, *refs):
    atts, owns, refs = refs[:tp], refs[tp : tp + 3], refs[tp + 3 :]
    pieces, outs, (cols_ref, xs_ref, w_ref, sem) = refs[: -tp - 4], refs[-tp - 4 : -4], refs[-4:]
    width, model = owns[0].shape
    rows, lanes = pieces[0].shape[1:]
    mine = at_ref[0] % 8
    copies = [pltpu.make_async_copy(ref, w_ref.at[i, pl.ds(0, width), :], sem.at[i]) for i, ref in enumerate(owns)]
    first = pieces[6].shape[0]
    for i, piece in enumerate(pieces):
        chip, start = (min(i // 2, 3), first if i // 2 == 4 else 0)
        place = mine ^ (2 * chip + i % 2)
        at = start
        while at < start + piece.shape[0]:
            unit, share = at // 3, at % 3
            size = min(3 - share, start + piece.shape[0] - at)
            row = pl.multiple_of((unit + 1) * width + (place // 2) * rows, 16)
            lane = pl.multiple_of((place % 2) * lanes, 128)
            target = w_ref.at[pl.ds(share, size), pl.ds(row, rows), pl.ds(lane, lanes)]
            copies.append(pltpu.make_async_copy(piece.at[pl.ds(at - start, size)], target, sem.at[len(copies)]))
            at += size
    for copy in copies:
        copy.start()
    half = x_ref.shape[1] // 2
    count = xl_ref.shape[0]
    xs_ref[...] = jnp.zeros_like(xs_ref)
    xs_ref[:count, :] = step_rows_of(xl_ref[...], at_ref[1])
    x = jnp.concatenate([x_ref[0].astype(F32), xs_ref[...]], axis=0)

    def rows_of(piece):
        tail = piece[half:].astype(F32)
        tail = jnp.concatenate([tail[:, :width], tail[:, width:]], axis=0).astype(BF16)
        return jnp.concatenate([piece[:half, :width], piece[:half, width:], tail], axis=0)

    attended = jnp.concatenate([rows_of(piece[...]) for piece in atts], axis=1)
    for copy in copies:
        copy.wait()
    mid = x + dot(attended, w_ref[0])
    normed = rms_scale(mid, gain_ref[...][None])
    pre = dot_t(normed, w_ref[1])
    hidden = (pre * (0.5 + 0.5 * jnp.tanh(0.5 * pre))).astype(BF16)
    out = mid + dot(hidden, w_ref[2])
    for b in range(tp):
        cols = out[:, b * width : (b + 1) * width]
        cols_ref[b, :half, :] = jnp.concatenate([cols[:half], cols[half : 2 * half]], axis=1).astype(BF16)
        tail = cols[2 * half :]
        cols_ref[b, half:, :] = jnp.concatenate([tail[: GROUP // 2], tail[GROUP // 2 :]], axis=1).astype(BF16)
    for k in range(tp):
        outs[k][...] = cols_ref[at_ref[1] ^ k]


def place_kernel(tp, at_ref, *refs):
    pieces, (short_ref, long_ref) = refs[:tp], refs[tp:]
    half, width = short_ref.shape[1] // 2, short_ref.shape[2]
    count = long_ref.shape[0]
    longs = jnp.zeros(long_ref.shape, F32)
    at = lax.broadcasted_iota(jnp.int32, longs.shape, 1)
    for k in range(tp):
        step = at_ref[1] ^ k
        short_ref[step, :half, :] = pieces[k][:half, :width]
        short_ref[step, half:, :] = pieces[k][:half, width:]
        tail = pieces[k][half:, :].astype(F32)
        tail = jnp.concatenate([tail[:, :width], tail[:, width:]], axis=0)[:count]
        longs = jnp.where(at == step, tail[:, None, :], longs)
    long_ref[...] = longs.astype(BF16)


def swap(value, axis, k):
    size = lax.axis_size(axis)
    return lax.ppermute(value, axis, [(i, i ^ k) for i in range(size)])


def whole(array):
    return pl.BlockSpec(array.shape, lambda *_: (0,) * array.ndim)


def call(kernel, at, operands, outs, specs=None, out_specs=None, grid=(1,), scratch=(), limit=16, flops=0, moved=1024, name=None):
    specs, out_specs = specs or {}, out_specs or {}
    return pl.pallas_call(
        kernel,
        grid_spec=pltpu.PrefetchScalarGridSpec(
            num_scalar_prefetch=1,
            grid=grid,
            in_specs=[specs.get(i, whole(a)) for i, a in enumerate(operands)],
            out_specs=[out_specs.get(i, whole(o)) for i, o in enumerate(outs)],
            scratch_shapes=list(scratch),
        ),
        out_shape=list(outs),
        compiler_params=pltpu.CompilerParams(vmem_limit_bytes=limit * MIB),
        cost_estimate=pl.CostEstimate(flops=flops, bytes_accessed=moved, transcendentals=0),
        name=name,
    )(at, *operands)


def per_device(
    short_inputs,
    long_inputs,
    short_keys,
    short_values,
    long_keys,
    long_values,
    short_lengths,
    long_lengths,
    attn_gain,
    mlp_gain,
    query_scale,
    q_weight,
    k_weight,
    v_weight,
    o_weight,
    up_weight,
    down_weight,
):
    steps, count, model = short_inputs.shape
    long_count = long_inputs.shape[1]
    heads, head_dim = query_scale.shape
    width = heads * head_dim
    tp, seq = lax.axis_size("tp"), lax.axis_size("seq")
    slots = short_keys.shape[1]
    at = jnp.stack([lax.axis_index("seq"), lax.axis_index("tp")]).astype(jnp.int32)
    shape = jax.ShapeDtypeStruct
    in_hbm = pl.BlockSpec(memory_space=pltpu.HBM)
    short_len, long_len = short_lengths, long_lengths
    long_rows_in = jnp.swapaxes(long_inputs, 0, 1)

    rows, lanes = width // 4, model // 2
    shares = (o_weight, up_weight.T, down_weight)
    eighth = pl.BlockSpec((rows, lanes), lambda _, at: ((at[0] % 8) // 2, at[0] % 2))
    (own,) = call(
        pack_kernel,
        at,
        shares,
        (shape((3, rows, lanes), BF16),),
        specs={0: eighth, 1: eighth, 2: eighth},
        limit=60,
        name="pack_weights",
    )
    units = [swap(own, "tp", k) for k in range(1, tp)]

    n = steps * GROUP
    step_rows = pl.BlockSpec((1, count, width), lambda i, at: (i, 0, 0))
    long_rows = pl.BlockSpec((1, GROUP, width), lambda i, at: (i, 0, 0))
    q, kn, vn, q_long, kn_long, vn_long = call(
        qkv_kernel,
        at,
        (short_inputs, long_rows_in, attn_gain, query_scale, q_weight.T, k_weight.T, v_weight.T),
        (shape((steps, count, width), BF16),) * 3 + (shape((steps, GROUP, width), BF16),) * 3,
        specs={
            0: pl.BlockSpec((1, count, model), lambda i, at: (i, 0, 0)),
            4: in_hbm,
            5: in_hbm,
            6: in_hbm,
        },
        out_specs={0: step_rows, 1: step_rows, 2: step_rows, 3: long_rows, 4: long_rows, 5: long_rows},
        grid=(steps,),
        scratch=(
            pltpu.VMEM((3 * width, model), BF16),
            pltpu.VMEM((count + GROUP, model), F32),
            pltpu.VMEM((steps, GROUP, model), F32),
            pltpu.SemaphoreType.DMA((3,)),
        ),
        limit=60,
        name="qkv",
    )

    part_shape = shape((n, width + 64), F32)
    (part,) = call(functools.partial(long_kernel, heads), at, (q_long, long_keys, long_values, long_len), (part_shape,), name="long_partial")
    (part,) = call(functools.partial(pair_kernel, heads, width), at, (part, swap(part, "seq", 1), units[0]), (part_shape,), specs={2: in_hbm}, name="long_pair")
    parts = [part] + [swap(part, "seq", 2 * i) for i in range(1, seq // 2)]

    block = count // 2
    packed = shape((count // 2 + GROUP // 2, 2 * width), BF16)
    fresh_rows = pl.BlockSpec((steps, block, width), lambda i, at: (0, i, 0))
    cache_rows = pl.BlockSpec((block, slots, width), lambda i, at: (i, 0, 0))
    (att,) = call(
        functools.partial(short_kernel, heads),
        at,
        (q, kn, vn, short_keys, short_values, short_len, part),
        (shape((steps, count, width), BF16),),
        specs={0: fresh_rows, 1: fresh_rows, 2: fresh_rows, 3: cache_rows, 4: cache_rows, 6: in_hbm},
        out_specs={0: fresh_rows},
        grid=(count // block,),
        limit=50,
        name="short_attention",
    )
    att_sent = call(
        functools.partial(send_kernel, heads),
        at,
        (att, q_long, kn_long, vn_long, *parts),
        (packed,) * steps,
        scratch=(pltpu.VMEM((steps, GROUP, width), F32), pltpu.VMEM((seq // 2, n, width + 64), F32)),
        name="send_attended",
    )
    received = [att_sent[0]] + [swap(att_sent[k], "tp", k) for k in range(1, tp)]

    blocks = 3 * (tp - 1)
    cut = blocks // 2 + 1
    (mine,) = call(
        functools.partial(stack_kernel, tp - 1),
        at,
        (*units, att, *parts[1:]),
        (shape((blocks, rows, lanes), BF16),),
        specs={tp - 1 + i: in_hbm for i in range(len(parts))},
        name="stack_weights",
    )
    along_x, along_y = swap(mine, "seq", 2), swap(mine, "seq", 4)
    first, second = call(
        functools.partial(cut_kernel, cut),
        at,
        (along_x, along_y, *received[1:]),
        (shape((cut, rows, lanes), BF16), shape((blocks - cut, rows, lanes), BF16)),
        specs={2 + i: in_hbm for i in range(tp - 1)},
        name="cut_weights",
    )
    spread = [mine, along_x, along_y, swap(first, "seq", 2), swap(second, "seq", 4)]
    pieces = [piece for held in spread for piece in (held, swap(held, "seq", 1))]

    outs = call(
        functools.partial(mlp_kernel, tp),
        at,
        (short_inputs, long_rows_in, mlp_gain, *received, *shares, *pieces),
        (packed,) * tp,
        specs={
            0: pl.BlockSpec((1, count, model), lambda _, at: (at[1], 0, 0)),
            **{3 + tp + i: in_hbm for i in range(3 + len(pieces))},
        },
        scratch=(
            pltpu.VMEM((tp, *packed.shape), BF16),
            pltpu.VMEM((GROUP, model), F32),
            pltpu.VMEM((3, tp * width, model), BF16),
            pltpu.SemaphoreType.DMA((3 + 9 * (tp - 1),)),
        ),
        flops=2 * (count + GROUP) * model * model * 3,
        limit=36,
        name="feed_forward",
    )
    outs = [outs[0]] + [swap(outs[k], "tp", k) for k in range(1, tp)]
    short_out, long_out = call(
        functools.partial(place_kernel, tp),
        at,
        outs,
        (shape((steps, count, width), BF16), shape((long_count, steps, width), BF16)),
        name="place_outputs",
    )
    return short_out, jnp.swapaxes(long_out, 0, 1)


def solution(mesh):
    return jax.shard_map(
        per_device,
        mesh=mesh,
        in_specs=(
            P(None, "seq", None),
            P(),
            P("seq", None, "tp"),
            P("seq", None, "tp"),
            P(None, "seq", "tp"),
            P(None, "seq", "tp"),
            P("seq"),
            P(),
            P(),
            P(),
            P("tp", None),
            P(None, "tp"),
            P(None, "tp"),
            P(None, "tp"),
            P("tp", None),
            P(None, "tp"),
            P("tp", None),
        ),
        out_specs=(P(None, "seq", "tp"), P(None, None, "tp")),
        check_vma=False,
    )
```

```python
import functools

import jax
import jax.numpy as jnp
from jax import lax
from jax.experimental import pallas as pl
from jax.experimental.pallas import tpu as pltpu
from jax.sharding import PartitionSpec as P

norm_eps = 1e-06
masked_fill = -1e30
GROUP = 16
F32 = jnp.float32
BF16 = jnp.bfloat16
MIB = 1024 * 1024


def rms_scale(rows, gain_row):
    mean_square = jnp.sum(rows * rows, axis=-1, keepdims=True) / rows.shape[-1]
    return (rows * lax.rsqrt(mean_square + norm_eps) * gain_row).astype(BF16)


def dot(a, b):
    return jnp.dot(a, b, preferred_element_type=F32)


def dot_t(a, b):
    return lax.dot_general(a, b, (((1,), (1,)), ((), ())), preferred_element_type=F32)


def lane_heads(rows, width, heads):
    return lax.broadcasted_iota(jnp.int32, (rows, width), 1) // (width // heads)


def stack_heads(queries, heads):
    head_of = lane_heads(*queries.shape, heads)
    return jnp.concatenate([jnp.where(head_of == h, queries, jnp.zeros_like(queries)) for h in range(heads)], axis=0)


def pick_heads(stacked, heads, width, head_dim=None):
    n = stacked.shape[0] // heads
    head_of = lax.broadcasted_iota(jnp.int32, (n, width), 1) // (head_dim or width // heads)
    picked = jnp.broadcast_to(stacked[:n], (n, width))
    for h in range(1, heads):
        picked = jnp.where(head_of == h, stacked[h * n : (h + 1) * n], picked)
    return picked


def slot_bias(lens, slots, columns):
    at = lax.broadcasted_iota(jnp.int32, (GROUP, columns), 1) - slots * lax.broadcasted_iota(jnp.int32, (GROUP, columns), 0)
    return jnp.where((at >= 0) & (at < lens), 0.0, masked_fill)


def fresh_bias(steps):
    n = steps * GROUP
    row = lax.broadcasted_iota(jnp.int32, (n, n), 0)
    col = lax.broadcasted_iota(jnp.int32, (n, n), 1)
    seen = (row % GROUP == col % GROUP) & (col // GROUP <= row // GROUP)
    return jnp.where(seen, 0.0, masked_fill)


def add_rows(scores, bias):
    reps = scores.shape[0] // bias.shape[0]
    return (scores.reshape(reps, *bias.shape) + bias[None]).reshape(scores.shape)


def pick_lens(len_row, base):
    lane = lax.broadcasted_iota(jnp.int32, (GROUP, len_row.shape[1]), 1)
    row = lax.broadcasted_iota(jnp.int32, (GROUP, len_row.shape[1]), 0)
    return jnp.sum(jnp.where(lane == base + row, len_row, 0), axis=1, keepdims=True)


def step_rows_of(rows, step):
    at = lax.broadcasted_iota(jnp.int32, rows.shape, 1)
    return jnp.sum(jnp.where(at == step, rows.astype(F32), 0.0), axis=1)


def scale_lanes(scale_ref):
    return jnp.concatenate([scale_ref[h : h + 1, :] for h in range(scale_ref.shape[0])], axis=1)


def qkv_kernel(at_ref, x_ref, xl_ref, gain_ref, scale_ref, qw_ref, kw_ref, vw_ref, fresh_ref, ql_ref, knl_ref, vnl_ref, w_ref, rows_ref, long_ref, sem):
    heads, head_dim = scale_ref.shape
    width = heads * head_dim
    short, count = x_ref.shape[1], xl_ref.shape[0]

    @pl.when(pl.program_id(0) == 0)
    def _():
        copies = [pltpu.make_async_copy(ref, w_ref.at[pl.ds(i * width, width), :], sem.at[i]) for i, ref in enumerate((qw_ref, kw_ref, vw_ref))]
        for copy in copies:
            copy.start()
        long_ref[...] = jnp.zeros_like(long_ref)
        for step in range(xl_ref.shape[1]):
            long_ref[step, :count, :] = xl_ref[:, step, :].astype(F32)
        for copy in copies:
            copy.wait()

    rows_ref[:short, :] = x_ref[0].astype(F32)
    rows_ref[short:, :] = long_ref[pl.program_id(0)]
    normed = rms_scale(rows_ref[...], gain_ref[...][None])
    product = dot_t(normed, w_ref[...])
    queries = (product[:, :width] * scale_lanes(scale_ref) * head_dim**-0.5).astype(BF16)
    keys = product[:, width : 2 * width].astype(BF16)
    values = product[:, 2 * width :].astype(BF16)
    for i, (rows, long_out) in enumerate(((queries, ql_ref), (keys, knl_ref), (values, vnl_ref))):
        fresh_ref[i, 0] = rows[:short]
        long_out[0] = rows[short:]


def put_sums(part_ref, row_max, weight_sum, width, heads):
    n = part_ref.shape[0]
    lane = lax.broadcasted_iota(jnp.int32, (n, part_ref.shape[1] - width), 1)
    tail = jnp.zeros(lane.shape, F32)
    for h in range(heads):
        tail = jnp.where(lane == h, row_max[h * n : (h + 1) * n], tail)
        tail = jnp.where(lane == heads + h, weight_sum[h * n : (h + 1) * n], tail)
    part_ref[:, width:] = tail


def get_column(part, first, heads):
    return jnp.concatenate([part[:, first + h : first + h + 1] for h in range(heads)], axis=0)


def long_kernel(heads, at_ref, q_ref, k_ref, v_ref, len_ref, part_ref):
    steps, _, width = q_ref.shape
    count, slots, _ = k_ref.shape
    n = steps * GROUP
    lens = jnp.minimum(pick_lens(len_ref[...][None], 0) - at_ref[0] * slots, slots)
    keys = k_ref[...].reshape(count * slots, width)
    values = v_ref[...].reshape(count * slots, width)
    bias = slot_bias(lens, slots, count * slots)
    scores = add_rows(dot_t(stack_heads(q_ref[...].reshape(n, width), heads), keys), bias)
    row_max = jnp.max(scores, axis=1, keepdims=True)
    probs = jnp.where(scores > 0.5 * masked_fill, jnp.exp(scores - row_max), 0.0)
    weight_sum = jnp.sum(probs, axis=1, keepdims=True)
    part_ref[:, :width] = pick_heads(dot(probs.astype(BF16), values), heads, width)
    put_sums(part_ref, row_max, weight_sum, width, heads)


def pair_kernel(heads, width, at_ref, mine_ref, other_ref, after_ref, out_ref):
    even = at_ref[0] % 2 == 0
    mine, other = mine_ref[...], other_ref[...]
    parts = (jnp.where(even, mine, other), jnp.where(even, other, mine))
    maxes = [get_column(part, width, heads) for part in parts]
    row_max = jnp.maximum(*maxes)
    weight_sum = jnp.zeros_like(row_max)
    acc = jnp.zeros((mine.shape[0], width), F32)
    for part, part_max in zip(parts, maxes):
        factor = jnp.exp(part_max - row_max)
        weight_sum = weight_sum + factor * get_column(part, width + heads, heads)
        acc = acc + part[:, :width] * pick_heads(factor, heads, width)
    out_ref[:, :width] = acc
    put_sums(out_ref, row_max, weight_sum, width, heads)


def merge_long(my_chip, parts, held_ref, q, kn, vn, heads):
    n, width = q.shape
    for i, part in enumerate(parts):
        held_ref[my_chip ^ i] = part[...]
    scores = add_rows(dot_t(stack_heads(q, heads), kn), fresh_bias(n // GROUP))
    total_max = jnp.max(scores, axis=1, keepdims=True)
    held = [held_ref[i] for i in range(len(parts))]
    maxes = [get_column(part, width, heads) for part in held]
    for part_max in maxes:
        total_max = jnp.maximum(total_max, part_max)
    probs = jnp.exp(scores - total_max)
    denom = jnp.sum(probs, axis=1, keepdims=True)
    acc = pick_heads(dot(probs.astype(BF16), vn), heads, width)
    for part, part_max in zip(held, maxes):
        factor = jnp.exp(part_max - total_max)
        denom = denom + factor * get_column(part, width + heads, heads)
        acc = acc + part[:, :width] * pick_heads(factor, heads, width)
    return acc / pick_heads(denom, heads, width)


def short_kernel(heads, at_ref, fresh_ref, k_ref, v_ref, len_ref, *refs):
    att_ref = refs[-1]
    _, steps, block, width = fresh_ref.shape
    slots = k_ref.shape[1]
    few = GROUP // 2
    n = steps * few
    cached = few * slots
    i = pl.program_id(0)
    row = lax.broadcasted_iota(jnp.int32, (n, n), 0)
    col = lax.broadcasted_iota(jnp.int32, (n, n), 1)
    seen = (row % few == col % few) & (col // few <= row // few)
    late = jnp.where(seen, 0.0, masked_fill)
    slot = lax.broadcasted_iota(jnp.int32, (few, cached), 1) - slots * lax.broadcasted_iota(jnp.int32, (few, cached), 0)
    lane = lax.broadcasted_iota(jnp.int32, (few, len_ref.shape[0]), 1)
    request = lax.broadcasted_iota(jnp.int32, (few, len_ref.shape[0]), 0)
    groups = range(block // few)
    queries, keys, values, biases = [], [], [], []
    for g in groups:
        at, lo = slice(g * few, (g + 1) * few), g // 2 * GROUP
        half = g % 2 * few
        new = [fresh_ref[j, :, lo : lo + GROUP, :].astype(F32)[:, half : half + few, :].reshape(n, width).astype(BF16) for j in range(3)]
        queries.append(stack_heads(new[0], heads))
        keys.append(jnp.concatenate([k_ref[at].reshape(cached, width), new[1]], axis=0))
        values.append(jnp.concatenate([v_ref[at].reshape(cached, width), new[2]], axis=0))
        lens = jnp.sum(jnp.where(lane == i * block + g * few + request, len_ref[...][None], 0), axis=1, keepdims=True)
        bias = jnp.where((slot >= 0) & (slot < lens), 0.0, masked_fill)
        biases.append(jnp.concatenate([jnp.concatenate([bias] * steps, axis=0), late], axis=1))
    scores = [add_rows(dot_t(queries[g], keys[g]), biases[g]) for g in groups]
    row_max = [jnp.max(scores[g], axis=1, keepdims=True) for g in groups]
    probs = [jnp.exp(scores[g] - row_max[g]) for g in groups]
    inverse = [1.0 / jnp.sum(probs[g], axis=1, keepdims=True) for g in groups]
    probs = [probs[g].astype(BF16) for g in groups]
    weighted = [dot(probs[g], values[g]) for g in groups]
    outs = [pick_heads(weighted[g] * inverse[g], heads, width) for g in groups]
    for g in groups[::2]:
        for s in range(steps):
            both = jnp.concatenate([outs[g][s * few : (s + 1) * few], outs[g + 1][s * few : (s + 1) * few]], axis=0)
            att_ref[s, g * few : (g + 2) * few, :] = both.astype(BF16)


def send_kernel(heads, at_ref, att_ref, ql_ref, knl_ref, vnl_ref, *refs):
    steps, count, width = att_ref.shape
    parts, outs, (long_ref, held_ref) = refs[: -2 - steps], refs[-2 - steps : -2], refs[-2:]
    half, n = count // 2, steps * GROUP
    longs = [ref[...].reshape(n, width) for ref in (ql_ref, knl_ref, vnl_ref)]
    merged = merge_long(at_ref[0] // 2, parts, held_ref, *longs, heads)
    for s in range(steps):
        long_ref[s] = merged[s * GROUP : (s + 1) * GROUP]
    for k in range(steps):
        rows = att_ref[at_ref[1] ^ k]
        mine = long_ref[at_ref[1] ^ k]
        outs[k][:half, :] = jnp.concatenate([rows[:half], rows[half:]], axis=1)
        outs[k][half:, :] = jnp.concatenate([mine[: GROUP // 2], mine[GROUP // 2 :]], axis=1).astype(BF16)


def pack_kernel(at_ref, o_ref, up_ref, down_ref, out_ref):
    for i, ref in enumerate((o_ref, up_ref, down_ref)):
        out_ref[i] = ref[...]


def stack_kernel(count, at_ref, *refs):
    for i in range(count):
        refs[-1][3 * i : 3 * i + 3] = refs[i][...]


def cut_kernel(cut, at_ref, x_ref, y_ref, *refs):
    refs[-2][...] = y_ref[:cut]
    refs[-1][...] = x_ref[cut:]


def mlp_kernel(tp, at_ref, x_ref, xl_ref, gain_ref, *refs):
    atts, owns, refs = refs[:tp], refs[tp : tp + 3], refs[tp + 3 :]
    pieces, outs, (cols_ref, xs_ref, w_ref, sem) = refs[: -tp - 4], refs[-tp - 4 : -4], refs[-4:]
    width, model = owns[0].shape
    rows, lanes = pieces[0].shape[1:]
    mine = at_ref[0] % 8
    copies = [pltpu.make_async_copy(ref, w_ref.at[i, pl.ds(0, width), :], sem.at[i]) for i, ref in enumerate(owns)]
    first = pieces[6].shape[0]
    for i, piece in enumerate(pieces):
        chip, start = (min(i // 2, 3), first if i // 2 == 4 else 0)
        place = mine ^ (2 * chip + i % 2)
        at = start
        while at < start + piece.shape[0]:
            unit, share = at // 3, at % 3
            size = min(3 - share, start + piece.shape[0] - at)
            row = pl.multiple_of((unit + 1) * width + (place // 2) * rows, 16)
            lane = pl.multiple_of((place % 2) * lanes, 128)
            target = w_ref.at[pl.ds(share, size), pl.ds(row, rows), pl.ds(lane, lanes)]
            copies.append(pltpu.make_async_copy(piece.at[pl.ds(at - start, size)], target, sem.at[len(copies)]))
            at += size
    for copy in copies:
        copy.start()
    half = x_ref.shape[1] // 2
    count = xl_ref.shape[0]
    xs_ref[...] = jnp.zeros_like(xs_ref)
    xs_ref[:count, :] = step_rows_of(xl_ref[...], at_ref[1])
    x = jnp.concatenate([x_ref[0].astype(F32), xs_ref[...]], axis=0)

    def rows_of(piece):
        tail = piece[half:].astype(F32)
        tail = jnp.concatenate([tail[:, :width], tail[:, width:]], axis=0).astype(BF16)
        return jnp.concatenate([piece[:half, :width], piece[:half, width:], tail], axis=0)

    attended = jnp.concatenate([rows_of(piece[...]) for piece in atts], axis=1)
    for copy in copies:
        copy.wait()
    mid = x + dot(attended, w_ref[0])
    normed = rms_scale(mid, gain_ref[...][None])
    pre = dot_t(normed, w_ref[1])
    hidden = (pre * (0.5 + 0.5 * jnp.tanh(0.5 * pre))).astype(BF16)
    out = mid + dot(hidden, w_ref[2])
    narrow = out[: 2 * half].astype(BF16)
    for b in range(tp):
        cols = narrow[:, b * width : (b + 1) * width]
        cols_ref[b, :half, :] = jnp.concatenate([cols[:half], cols[half:]], axis=1)
        tail = out[2 * half :, b * width : (b + 1) * width]
        cols_ref[b, half:, :] = jnp.concatenate([tail[: GROUP // 2], tail[GROUP // 2 :]], axis=1).astype(BF16)
    for k in range(tp):
        outs[k][...] = cols_ref[at_ref[1] ^ k]


def place_kernel(tp, at_ref, *refs):
    pieces, (short_ref, long_ref) = refs[:tp], refs[tp:]
    half, width = short_ref.shape[1] // 2, short_ref.shape[2]
    count = long_ref.shape[0]
    longs = jnp.zeros(long_ref.shape, F32)
    at = lax.broadcasted_iota(jnp.int32, longs.shape, 1)
    for k in range(tp):
        step = at_ref[1] ^ k
        short_ref[step, :half, :] = pieces[k][:half, :width]
        short_ref[step, half:, :] = pieces[k][:half, width:]
        tail = pieces[k][half:, :].astype(F32)
        tail = jnp.concatenate([tail[:, :width], tail[:, width:]], axis=0)[:count]
        longs = jnp.where(at == step, tail[:, None, :], longs)
    long_ref[...] = longs.astype(BF16)


def swap(value, axis, k):
    size = lax.axis_size(axis)
    return lax.ppermute(value, axis, [(i, i ^ k) for i in range(size)])


def whole(array):
    return pl.BlockSpec(array.shape, lambda *_: (0,) * array.ndim)


def call(kernel, at, operands, outs, specs=None, out_specs=None, grid=(1,), scratch=(), limit=16, flops=0, moved=1024, name=None):
    specs, out_specs = specs or {}, out_specs or {}
    return pl.pallas_call(
        kernel,
        grid_spec=pltpu.PrefetchScalarGridSpec(
            num_scalar_prefetch=1,
            grid=grid,
            in_specs=[specs.get(i, whole(a)) for i, a in enumerate(operands)],
            out_specs=[out_specs.get(i, whole(o)) for i, o in enumerate(outs)],
            scratch_shapes=list(scratch),
        ),
        out_shape=list(outs),
        compiler_params=pltpu.CompilerParams(vmem_limit_bytes=limit * MIB),
        cost_estimate=pl.CostEstimate(flops=flops, bytes_accessed=moved, transcendentals=0),
        name=name,
    )(at, *operands)


def per_device(
    short_inputs,
    long_inputs,
    short_keys,
    short_values,
    long_keys,
    long_values,
    short_lengths,
    long_lengths,
    attn_gain,
    mlp_gain,
    query_scale,
    q_weight,
    k_weight,
    v_weight,
    o_weight,
    up_weight,
    down_weight,
):
    steps, count, model = short_inputs.shape
    long_count = long_inputs.shape[1]
    heads, head_dim = query_scale.shape
    width = heads * head_dim
    tp, seq = lax.axis_size("tp"), lax.axis_size("seq")
    slots = short_keys.shape[1]
    at = jnp.stack([lax.axis_index("seq"), lax.axis_index("tp")]).astype(jnp.int32)
    shape = jax.ShapeDtypeStruct
    in_hbm = pl.BlockSpec(memory_space=pltpu.HBM)
    short_len, long_len = short_lengths, long_lengths
    long_rows_in = jnp.swapaxes(long_inputs, 0, 1)

    rows, lanes = width // 4, model // 2
    shares = (o_weight, up_weight.T, down_weight)
    eighth = pl.BlockSpec((rows, lanes), lambda _, at: ((at[0] % 8) // 2, at[0] % 2))
    (own,) = call(
        pack_kernel,
        at,
        shares,
        (shape((3, rows, lanes), BF16),),
        specs={0: eighth, 1: eighth, 2: eighth},
        limit=60,
        name="pack_weights",
    )
    units = [swap(own, "tp", k) for k in range(1, tp)]

    n = steps * GROUP
    step_rows = pl.BlockSpec((3, 1, count, width), lambda i, at: (0, i, 0, 0))
    long_rows = pl.BlockSpec((1, GROUP, width), lambda i, at: (i, 0, 0))
    fresh, q_long, kn_long, vn_long = call(
        qkv_kernel,
        at,
        (short_inputs, long_rows_in, attn_gain, query_scale, q_weight.T, k_weight.T, v_weight.T),
        (shape((3, steps, count, width), BF16),) + (shape((steps, GROUP, width), BF16),) * 3,
        specs={
            0: pl.BlockSpec((1, count, model), lambda i, at: (i, 0, 0)),
            4: in_hbm,
            5: in_hbm,
            6: in_hbm,
        },
        out_specs={0: step_rows, 1: long_rows, 2: long_rows, 3: long_rows},
        grid=(steps,),
        scratch=(
            pltpu.VMEM((3 * width, model), BF16),
            pltpu.VMEM((count + GROUP, model), F32),
            pltpu.VMEM((steps, GROUP, model), F32),
            pltpu.SemaphoreType.DMA((3,)),
        ),
        limit=60,
        name="qkv",
    )

    part_shape = shape((n, width + 64), F32)
    (part,) = call(functools.partial(long_kernel, heads), at, (q_long, long_keys, long_values, long_len), (part_shape,), name="long_partial")
    (part,) = call(functools.partial(pair_kernel, heads, width), at, (part, swap(part, "seq", 1), units[0]), (part_shape,), specs={2: in_hbm}, name="long_pair")
    parts = [part] + [swap(part, "seq", 2 * i) for i in range(1, seq // 2)]

    block = count // 2
    packed = shape((count // 2 + GROUP // 2, 2 * width), BF16)
    fresh_rows = pl.BlockSpec((steps, block, width), lambda i, at: (0, i, 0))
    cache_rows = pl.BlockSpec((block, slots, width), lambda i, at: (i, 0, 0))
    (att,) = call(
        functools.partial(short_kernel, heads),
        at,
        (fresh, short_keys, short_values, short_len, part),
        (shape((steps, count, width), BF16),),
        specs={0: pl.BlockSpec((3, steps, block, width), lambda i, at: (0, 0, i, 0)), 1: cache_rows, 2: cache_rows, 4: in_hbm},
        out_specs={0: fresh_rows},
        grid=(count // block,),
        limit=50,
        name="short_attention",
    )
    att_sent = call(
        functools.partial(send_kernel, heads),
        at,
        (att, q_long, kn_long, vn_long, *parts),
        (packed,) * steps,
        scratch=(pltpu.VMEM((steps, GROUP, width), F32), pltpu.VMEM((seq // 2, n, width + 64), F32)),
        name="send_attended",
    )
    received = [att_sent[0]] + [swap(att_sent[k], "tp", k) for k in range(1, tp)]

    blocks = 3 * (tp - 1)
    cut = blocks // 2 + 1
    (mine,) = call(
        functools.partial(stack_kernel, tp - 1),
        at,
        (*units, att, *parts[1:]),
        (shape((blocks, rows, lanes), BF16),),
        specs={tp - 1 + i: in_hbm for i in range(len(parts))},
        name="stack_weights",
    )
    along_x, along_y = swap(mine, "seq", 2), swap(mine, "seq", 4)
    first, second = call(
        functools.partial(cut_kernel, cut),
        at,
        (along_x, along_y, *received[1:]),
        (shape((cut, rows, lanes), BF16), shape((blocks - cut, rows, lanes), BF16)),
        specs={2 + i: in_hbm for i in range(tp - 1)},
        name="cut_weights",
    )
    spread = [mine, along_x, along_y, swap(first, "seq", 2), swap(second, "seq", 4)]
    pieces = [piece for held in spread for piece in (held, swap(held, "seq", 1))]

    outs = call(
        functools.partial(mlp_kernel, tp),
        at,
        (short_inputs, long_rows_in, mlp_gain, *received, *shares, *pieces),
        (packed,) * tp,
        specs={
            0: pl.BlockSpec((1, count, model), lambda _, at: (at[1], 0, 0)),
            **{3 + tp + i: in_hbm for i in range(3 + len(pieces))},
        },
        scratch=(
            pltpu.VMEM((tp, *packed.shape), BF16),
            pltpu.VMEM((GROUP, model), F32),
            pltpu.VMEM((3, tp * width, model), BF16),
            pltpu.SemaphoreType.DMA((3 + 9 * (tp - 1),)),
        ),
        flops=2 * (count + GROUP) * model * model * 3,
        limit=36,
        name="feed_forward",
    )
    outs = [outs[0]] + [swap(outs[k], "tp", k) for k in range(1, tp)]
    short_out, long_out = call(
        functools.partial(place_kernel, tp),
        at,
        outs,
        (shape((steps, count, width), BF16), shape((long_count, steps, width), BF16)),
        name="place_outputs",
    )
    return short_out, jnp.swapaxes(long_out, 0, 1)


def solution(mesh):
    return jax.shard_map(
        per_device,
        mesh=mesh,
        in_specs=(
            P(None, "seq", None),
            P(),
            P("seq", None, "tp"),
            P("seq", None, "tp"),
            P(None, "seq", "tp"),
            P(None, "seq", "tp"),
            P("seq"),
            P(),
            P(),
            P(),
            P("tp", None),
            P(None, "tp"),
            P(None, "tp"),
            P(None, "tp"),
            P("tp", None),
            P(None, "tp"),
            P("tp", None),
        ),
        out_specs=(P(None, "seq", "tp"), P(None, None, "tp")),
        check_vma=False,
    )
```

```python
import functools

import jax
import jax.numpy as jnp
from jax import lax
from jax.experimental import pallas as pl
from jax.experimental.pallas import tpu as pltpu
from jax.sharding import PartitionSpec as P

norm_eps = 1e-06
masked_fill = -1e30
GROUP = 16
F32 = jnp.float32
BF16 = jnp.bfloat16
MIB = 1024 * 1024


def rms_scale(rows, gain_row):
    mean_square = jnp.sum(rows * rows, axis=-1, keepdims=True) / rows.shape[-1]
    return (rows * lax.rsqrt(mean_square + norm_eps) * gain_row).astype(BF16)


def dot(a, b):
    return jnp.dot(a, b, preferred_element_type=F32)


def dot_t(a, b):
    return lax.dot_general(a, b, (((1,), (1,)), ((), ())), preferred_element_type=F32)


def lane_heads(rows, width, heads):
    return lax.broadcasted_iota(jnp.int32, (rows, width), 1) // (width // heads)


def stack_heads(queries, heads):
    head_of = lane_heads(*queries.shape, heads)
    return jnp.concatenate([jnp.where(head_of == h, queries, jnp.zeros_like(queries)) for h in range(heads)], axis=0)


def pick_heads(stacked, heads, width, head_dim=None):
    n = stacked.shape[0] // heads
    head_of = lax.broadcasted_iota(jnp.int32, (n, width), 1) // (head_dim or width // heads)
    picked = jnp.broadcast_to(stacked[:n], (n, width))
    for h in range(1, heads):
        picked = jnp.where(head_of == h, stacked[h * n : (h + 1) * n], picked)
    return picked


def slot_bias(lens, slots, columns):
    at = lax.broadcasted_iota(jnp.int32, (GROUP, columns), 1) - slots * lax.broadcasted_iota(jnp.int32, (GROUP, columns), 0)
    return jnp.where((at >= 0) & (at < lens), 0.0, masked_fill)


def fresh_bias(steps):
    n = steps * GROUP
    row = lax.broadcasted_iota(jnp.int32, (n, n), 0)
    col = lax.broadcasted_iota(jnp.int32, (n, n), 1)
    seen = (row % GROUP == col % GROUP) & (col // GROUP <= row // GROUP)
    return jnp.where(seen, 0.0, masked_fill)


def add_rows(scores, bias):
    reps = scores.shape[0] // bias.shape[0]
    return (scores.reshape(reps, *bias.shape) + bias[None]).reshape(scores.shape)


def pick_lens(len_row, base):
    lane = lax.broadcasted_iota(jnp.int32, (GROUP, len_row.shape[1]), 1)
    row = lax.broadcasted_iota(jnp.int32, (GROUP, len_row.shape[1]), 0)
    return jnp.sum(jnp.where(lane == base + row, len_row, 0), axis=1, keepdims=True)


def step_rows_of(rows, step):
    at = lax.broadcasted_iota(jnp.int32, rows.shape, 1)
    return jnp.sum(jnp.where(at == step, rows.astype(F32), 0.0), axis=1)


def scale_lanes(scale_ref):
    return jnp.concatenate([scale_ref[h : h + 1, :] for h in range(scale_ref.shape[0])], axis=1)


def qkv_kernel(at_ref, x_ref, xl_ref, gain_ref, scale_ref, qw_ref, kw_ref, vw_ref, fresh_ref, ql_ref, knl_ref, vnl_ref, w_ref, rows_ref, long_ref, sem):
    heads, head_dim = scale_ref.shape
    width = heads * head_dim
    short, count = x_ref.shape[1], xl_ref.shape[0]

    @pl.when(pl.program_id(0) == 0)
    def _():
        copies = [pltpu.make_async_copy(ref, w_ref.at[pl.ds(i * width, width), :], sem.at[i]) for i, ref in enumerate((qw_ref, kw_ref, vw_ref))]
        for copy in copies:
            copy.start()
        long_ref[...] = jnp.zeros_like(long_ref)
        for step in range(xl_ref.shape[1]):
            long_ref[step, :count, :] = xl_ref[:, step, :].astype(F32)
        for copy in copies:
            copy.wait()

    rows_ref[:short, :] = x_ref[0].astype(F32)
    rows_ref[short:, :] = long_ref[pl.program_id(0)]
    normed = rms_scale(rows_ref[...], gain_ref[...][None])
    product = dot_t(normed, w_ref[...])
    queries = (product[:, :width] * scale_lanes(scale_ref) * head_dim**-0.5).astype(BF16)
    keys = product[:, width : 2 * width].astype(BF16)
    values = product[:, 2 * width :].astype(BF16)
    for i, (rows, long_out) in enumerate(((queries, ql_ref), (keys, knl_ref), (values, vnl_ref))):
        fresh_ref[i, 0] = rows[:short]
        long_out[0] = rows[short:]


def put_sums(part_ref, row_max, weight_sum, width, heads):
    n = part_ref.shape[0]
    lane = lax.broadcasted_iota(jnp.int32, (n, part_ref.shape[1] - width), 1)
    tail = jnp.zeros(lane.shape, F32)
    for h in range(heads):
        tail = jnp.where(lane == h, row_max[h * n : (h + 1) * n], tail)
        tail = jnp.where(lane == heads + h, weight_sum[h * n : (h + 1) * n], tail)
    part_ref[:, width:] = tail


def get_column(part, first, heads):
    return jnp.concatenate([part[:, first + h : first + h + 1] for h in range(heads)], axis=0)


def long_kernel(heads, at_ref, q_ref, k_ref, v_ref, len_ref, part_ref):
    steps, _, width = q_ref.shape
    count, slots, _ = k_ref.shape
    n = steps * GROUP
    lens = jnp.minimum(pick_lens(len_ref[...][None], 0) - at_ref[0] * slots, slots)
    keys = k_ref[...].reshape(count * slots, width)
    values = v_ref[...].reshape(count * slots, width)
    bias = slot_bias(lens, slots, count * slots)
    scores = add_rows(dot_t(stack_heads(q_ref[...].reshape(n, width), heads), keys), bias)
    row_max = jnp.max(scores, axis=1, keepdims=True)
    probs = jnp.where(scores > 0.5 * masked_fill, jnp.exp(scores - row_max), 0.0)
    weight_sum = jnp.sum(probs, axis=1, keepdims=True)
    part_ref[:, :width] = pick_heads(dot(probs.astype(BF16), values), heads, width)
    put_sums(part_ref, row_max, weight_sum, width, heads)


def pair_kernel(heads, width, at_ref, mine_ref, other_ref, after_ref, out_ref):
    even = at_ref[0] % 2 == 0
    mine, other = mine_ref[...], other_ref[...]
    parts = (jnp.where(even, mine, other), jnp.where(even, other, mine))
    maxes = [get_column(part, width, heads) for part in parts]
    row_max = jnp.maximum(*maxes)
    weight_sum = jnp.zeros_like(row_max)
    acc = jnp.zeros((mine.shape[0], width), F32)
    for part, part_max in zip(parts, maxes):
        factor = jnp.exp(part_max - row_max)
        weight_sum = weight_sum + factor * get_column(part, width + heads, heads)
        acc = acc + part[:, :width] * pick_heads(factor, heads, width)
    out_ref[:, :width] = acc
    put_sums(out_ref, row_max, weight_sum, width, heads)


def merge_long(my_chip, parts, held_ref, q, kn, vn, heads):
    n, width = q.shape
    for i, part in enumerate(parts):
        held_ref[my_chip ^ i] = part[...]
    scores = add_rows(dot_t(stack_heads(q, heads), kn), fresh_bias(n // GROUP))
    total_max = jnp.max(scores, axis=1, keepdims=True)
    held = [held_ref[i] for i in range(len(parts))]
    maxes = [get_column(part, width, heads) for part in held]
    for part_max in maxes:
        total_max = jnp.maximum(total_max, part_max)
    probs = jnp.exp(scores - total_max)
    denom = jnp.sum(probs, axis=1, keepdims=True)
    acc = pick_heads(dot(probs.astype(BF16), vn), heads, width)
    for part, part_max in zip(held, maxes):
        factor = jnp.exp(part_max - total_max)
        denom = denom + factor * get_column(part, width + heads, heads)
        acc = acc + part[:, :width] * pick_heads(factor, heads, width)
    return acc / pick_heads(denom, heads, width)


def short_kernel(heads, at_ref, fresh_ref, k_ref, v_ref, len_ref, *refs):
    att_ref = refs[-1]
    _, steps, block, width = fresh_ref.shape
    slots = k_ref.shape[1]
    few = GROUP // 2
    n = steps * few
    cached = few * slots
    i = pl.program_id(0)
    row = lax.broadcasted_iota(jnp.int32, (n, n), 0)
    col = lax.broadcasted_iota(jnp.int32, (n, n), 1)
    seen = (row % few == col % few) & (col // few <= row // few)
    late = jnp.where(seen, 0.0, masked_fill)
    slot = lax.broadcasted_iota(jnp.int32, (few, cached), 1) - slots * lax.broadcasted_iota(jnp.int32, (few, cached), 0)
    lane = lax.broadcasted_iota(jnp.int32, (few, len_ref.shape[0]), 1)
    request = lax.broadcasted_iota(jnp.int32, (few, len_ref.shape[0]), 0)
    groups = range(block // few)
    queries, keys, values, biases = [], [], [], []
    for g in groups:
        at, lo = slice(g * few, (g + 1) * few), g // 2 * GROUP
        half = g % 2 * few
        new = [fresh_ref[j, :, lo : lo + GROUP, :].astype(F32)[:, half : half + few, :].reshape(n, width).astype(BF16) for j in range(3)]
        queries.append(stack_heads(new[0], heads))
        keys.append(jnp.concatenate([k_ref[at].reshape(cached, width), new[1]], axis=0))
        values.append(jnp.concatenate([v_ref[at].reshape(cached, width), new[2]], axis=0))
        lens = jnp.sum(jnp.where(lane == i * block + g * few + request, len_ref[...][None], 0), axis=1, keepdims=True)
        bias = jnp.where((slot >= 0) & (slot < lens), 0.0, masked_fill)
        biases.append(jnp.concatenate([jnp.concatenate([bias] * steps, axis=0), late], axis=1))
    scores = [add_rows(dot_t(queries[g], keys[g]), biases[g]) for g in groups]
    row_max = [jnp.max(scores[g], axis=1, keepdims=True) for g in groups]
    probs = [jnp.exp(scores[g] - row_max[g]) for g in groups]
    inverse = [1.0 / jnp.sum(probs[g], axis=1, keepdims=True) for g in groups]
    probs = [probs[g].astype(BF16) for g in groups]
    weighted = [dot(probs[g], values[g]) for g in groups]
    outs = [pick_heads(weighted[g] * inverse[g], heads, width) for g in groups]
    for g in groups[::2]:
        for s in range(steps):
            both = jnp.concatenate([outs[g][s * few : (s + 1) * few], outs[g + 1][s * few : (s + 1) * few]], axis=0)
            att_ref[s, g * few : (g + 2) * few, :] = both.astype(BF16)


def send_kernel(heads, at_ref, att_ref, ql_ref, knl_ref, vnl_ref, *refs):
    steps, count, width = att_ref.shape
    parts, outs, (long_ref, held_ref) = refs[: -2 - steps], refs[-2 - steps : -2], refs[-2:]
    half, n = count // 2, steps * GROUP
    longs = [ref[...].reshape(n, width) for ref in (ql_ref, knl_ref, vnl_ref)]
    merged = merge_long(at_ref[0] // 2, parts, held_ref, *longs, heads)
    for s in range(steps):
        long_ref[s] = merged[s * GROUP : (s + 1) * GROUP]
    for k in range(steps):
        rows = att_ref[at_ref[1] ^ k]
        mine = long_ref[at_ref[1] ^ k]
        outs[k][:half, :] = jnp.concatenate([rows[:half], rows[half:]], axis=1)
        outs[k][half:, :] = jnp.concatenate([mine, jnp.zeros_like(mine)], axis=1).astype(BF16)


def pack_kernel(at_ref, o_ref, up_ref, down_ref, out_ref):
    for i, ref in enumerate((o_ref, up_ref, down_ref)):
        out_ref[i] = ref[...]


def stack_kernel(count, at_ref, *refs):
    for i in range(count):
        refs[-1][3 * i : 3 * i + 3] = refs[i][...]


def cut_kernel(cut, at_ref, x_ref, y_ref, *refs):
    refs[-2][...] = y_ref[:cut]
    refs[-1][...] = x_ref[cut:]


def mlp_kernel(tp, at_ref, x_ref, xl_ref, gain_ref, *refs):
    atts, owns, refs = refs[:tp], refs[tp : tp + 3], refs[tp + 3 :]
    pieces, outs, (cols_ref, xs_ref, w_ref, sem) = refs[: -tp - 4], refs[-tp - 4 : -4], refs[-4:]
    width, model = owns[0].shape
    rows, lanes = pieces[0].shape[1:]
    mine = at_ref[0] % 8
    copies = [pltpu.make_async_copy(ref, w_ref.at[i, pl.ds(0, width), :], sem.at[i]) for i, ref in enumerate(owns)]
    first = pieces[6].shape[0]
    for i, piece in enumerate(pieces):
        chip, start = (min(i // 2, 3), first if i // 2 == 4 else 0)
        place = mine ^ (2 * chip + i % 2)
        at = start
        while at < start + piece.shape[0]:
            unit, share = at // 3, at % 3
            size = min(3 - share, start + piece.shape[0] - at)
            row = pl.multiple_of((unit + 1) * width + (place // 2) * rows, 16)
            lane = pl.multiple_of((place % 2) * lanes, 128)
            target = w_ref.at[pl.ds(share, size), pl.ds(row, rows), pl.ds(lane, lanes)]
            copies.append(pltpu.make_async_copy(piece.at[pl.ds(at - start, size)], target, sem.at[len(copies)]))
            at += size
    for copy in copies:
        copy.start()
    half = x_ref.shape[1] // 2
    count = xl_ref.shape[0]
    xs_ref[...] = jnp.zeros_like(xs_ref)
    xs_ref[:count, :] = step_rows_of(xl_ref[...], at_ref[1])
    x = jnp.concatenate([x_ref[0].astype(F32), xs_ref[...]], axis=0)

    def rows_of(piece):
        return jnp.concatenate([piece[:half, :width], piece[:half, width:], piece[half:, :width]], axis=0)

    attended = jnp.concatenate([rows_of(piece[...]) for piece in atts], axis=1)
    for copy in copies:
        copy.wait()
    mid = x + dot(attended, w_ref[0])
    normed = rms_scale(mid, gain_ref[...][None])
    pre = dot_t(normed, w_ref[1])
    hidden = (pre * (0.5 + 0.5 * jnp.tanh(0.5 * pre))).astype(BF16)
    out = mid + dot(hidden, w_ref[2])
    narrow = out[: 2 * half].astype(BF16)
    for b in range(tp):
        cols = narrow[:, b * width : (b + 1) * width]
        cols_ref[b, :half, :] = jnp.concatenate([cols[:half], cols[half:]], axis=1)
        tail = out[2 * half :, b * width : (b + 1) * width]
        cols_ref[b, half:, :] = jnp.concatenate([tail, jnp.zeros_like(tail)], axis=1).astype(BF16)
    for k in range(tp):
        outs[k][...] = cols_ref[at_ref[1] ^ k]


def place_kernel(tp, at_ref, *refs):
    pieces, (short_ref, long_ref) = refs[:tp], refs[tp:]
    half, width = short_ref.shape[1] // 2, short_ref.shape[2]
    count = long_ref.shape[0]
    longs = jnp.zeros(long_ref.shape, F32)
    at = lax.broadcasted_iota(jnp.int32, longs.shape, 1)
    for k in range(tp):
        step = at_ref[1] ^ k
        short_ref[step, :half, :] = pieces[k][:half, :width]
        short_ref[step, half:, :] = pieces[k][:half, width:]
        tail = pieces[k][half:, :width].astype(F32)[:count]
        longs = jnp.where(at == step, tail[:, None, :], longs)
    long_ref[...] = longs.astype(BF16)


def swap(value, axis, k):
    size = lax.axis_size(axis)
    return lax.ppermute(value, axis, [(i, i ^ k) for i in range(size)])


def whole(array):
    return pl.BlockSpec(array.shape, lambda *_: (0,) * array.ndim)


def call(kernel, at, operands, outs, specs=None, out_specs=None, grid=(1,), scratch=(), limit=16, flops=0, moved=1024, name=None):
    specs, out_specs = specs or {}, out_specs or {}
    return pl.pallas_call(
        kernel,
        grid_spec=pltpu.PrefetchScalarGridSpec(
            num_scalar_prefetch=1,
            grid=grid,
            in_specs=[specs.get(i, whole(a)) for i, a in enumerate(operands)],
            out_specs=[out_specs.get(i, whole(o)) for i, o in enumerate(outs)],
            scratch_shapes=list(scratch),
        ),
        out_shape=list(outs),
        compiler_params=pltpu.CompilerParams(vmem_limit_bytes=limit * MIB),
        cost_estimate=pl.CostEstimate(flops=flops, bytes_accessed=moved, transcendentals=0),
        name=name,
    )(at, *operands)


def per_device(
    short_inputs,
    long_inputs,
    short_keys,
    short_values,
    long_keys,
    long_values,
    short_lengths,
    long_lengths,
    attn_gain,
    mlp_gain,
    query_scale,
    q_weight,
    k_weight,
    v_weight,
    o_weight,
    up_weight,
    down_weight,
):
    steps, count, model = short_inputs.shape
    long_count = long_inputs.shape[1]
    heads, head_dim = query_scale.shape
    width = heads * head_dim
    tp, seq = lax.axis_size("tp"), lax.axis_size("seq")
    slots = short_keys.shape[1]
    at = jnp.stack([lax.axis_index("seq"), lax.axis_index("tp")]).astype(jnp.int32)
    shape = jax.ShapeDtypeStruct
    in_hbm = pl.BlockSpec(memory_space=pltpu.HBM)
    short_len, long_len = short_lengths, long_lengths
    long_rows_in = jnp.swapaxes(long_inputs, 0, 1)

    rows, lanes = width // 4, model // 2
    shares = (o_weight, up_weight.T, down_weight)
    eighth = pl.BlockSpec((rows, lanes), lambda _, at: ((at[0] % 8) // 2, at[0] % 2))
    (own,) = call(
        pack_kernel,
        at,
        shares,
        (shape((3, rows, lanes), BF16),),
        specs={0: eighth, 1: eighth, 2: eighth},
        limit=60,
        name="pack_weights",
    )
    units = [swap(own, "tp", k) for k in range(1, tp)]

    n = steps * GROUP
    step_rows = pl.BlockSpec((3, 1, count, width), lambda i, at: (0, i, 0, 0))
    long_rows = pl.BlockSpec((1, GROUP, width), lambda i, at: (i, 0, 0))
    fresh, q_long, kn_long, vn_long = call(
        qkv_kernel,
        at,
        (short_inputs, long_rows_in, attn_gain, query_scale, q_weight.T, k_weight.T, v_weight.T),
        (shape((3, steps, count, width), BF16),) + (shape((steps, GROUP, width), BF16),) * 3,
        specs={
            0: pl.BlockSpec((1, count, model), lambda i, at: (i, 0, 0)),
            4: in_hbm,
            5: in_hbm,
            6: in_hbm,
        },
        out_specs={0: step_rows, 1: long_rows, 2: long_rows, 3: long_rows},
        grid=(steps,),
        scratch=(
            pltpu.VMEM((3 * width, model), BF16),
            pltpu.VMEM((count + GROUP, model), F32),
            pltpu.VMEM((steps, GROUP, model), F32),
            pltpu.SemaphoreType.DMA((3,)),
        ),
        limit=60,
        name="qkv",
    )

    part_shape = shape((n, width + 64), F32)
    (part,) = call(functools.partial(long_kernel, heads), at, (q_long, long_keys, long_values, long_len), (part_shape,), name="long_partial")
    (part,) = call(functools.partial(pair_kernel, heads, width), at, (part, swap(part, "seq", 1), units[0]), (part_shape,), specs={2: in_hbm}, name="long_pair")
    parts = [part] + [swap(part, "seq", 2 * i) for i in range(1, seq // 2)]

    block = count // 2
    packed = shape((count // 2 + GROUP, 2 * width), BF16)
    fresh_rows = pl.BlockSpec((steps, block, width), lambda i, at: (0, i, 0))
    cache_rows = pl.BlockSpec((block, slots, width), lambda i, at: (i, 0, 0))
    (att,) = call(
        functools.partial(short_kernel, heads),
        at,
        (fresh, short_keys, short_values, short_len, part),
        (shape((steps, count, width), BF16),),
        specs={0: pl.BlockSpec((3, steps, block, width), lambda i, at: (0, 0, i, 0)), 1: cache_rows, 2: cache_rows, 4: in_hbm},
        out_specs={0: fresh_rows},
        grid=(count // block,),
        limit=50,
        name="short_attention",
    )
    att_sent = call(
        functools.partial(send_kernel, heads),
        at,
        (att, q_long, kn_long, vn_long, *parts),
        (packed,) * steps,
        scratch=(pltpu.VMEM((steps, GROUP, width), F32), pltpu.VMEM((seq // 2, n, width + 64), F32)),
        name="send_attended",
    )
    received = [att_sent[0]] + [swap(att_sent[k], "tp", k) for k in range(1, tp)]

    blocks = 3 * (tp - 1)
    cut = blocks // 2 + 1
    (mine,) = call(
        functools.partial(stack_kernel, tp - 1),
        at,
        (*units, att, *parts[1:]),
        (shape((blocks, rows, lanes), BF16),),
        specs={tp - 1 + i: in_hbm for i in range(len(parts))},
        name="stack_weights",
    )
    along_x, along_y = swap(mine, "seq", 2), swap(mine, "seq", 4)
    first, second = call(
        functools.partial(cut_kernel, cut),
        at,
        (along_x, along_y, *received[1:]),
        (shape((cut, rows, lanes), BF16), shape((blocks - cut, rows, lanes), BF16)),
        specs={2 + i: in_hbm for i in range(tp - 1)},
        name="cut_weights",
    )
    spread = [mine, along_x, along_y, swap(first, "seq", 2), swap(second, "seq", 4)]
    pieces = [piece for held in spread for piece in (held, swap(held, "seq", 1))]

    outs = call(
        functools.partial(mlp_kernel, tp),
        at,
        (short_inputs, long_rows_in, mlp_gain, *received, *shares, *pieces),
        (packed,) * tp,
        specs={
            0: pl.BlockSpec((1, count, model), lambda _, at: (at[1], 0, 0)),
            **{3 + tp + i: in_hbm for i in range(3 + len(pieces))},
        },
        scratch=(
            pltpu.VMEM((tp, *packed.shape), BF16),
            pltpu.VMEM((GROUP, model), F32),
            pltpu.VMEM((3, tp * width, model), BF16),
            pltpu.SemaphoreType.DMA((3 + 9 * (tp - 1),)),
        ),
        flops=2 * (count + GROUP) * model * model * 3,
        limit=36,
        name="feed_forward",
    )
    outs = [outs[0]] + [swap(outs[k], "tp", k) for k in range(1, tp)]
    short_out, long_out = call(
        functools.partial(place_kernel, tp),
        at,
        outs,
        (shape((steps, count, width), BF16), shape((long_count, steps, width), BF16)),
        name="place_outputs",
    )
    return short_out, jnp.swapaxes(long_out, 0, 1)


def solution(mesh):
    return jax.shard_map(
        per_device,
        mesh=mesh,
        in_specs=(
            P(None, "seq", None),
            P(),
            P("seq", None, "tp"),
            P("seq", None, "tp"),
            P(None, "seq", "tp"),
            P(None, "seq", "tp"),
            P("seq"),
            P(),
            P(),
            P(),
            P("tp", None),
            P(None, "tp"),
            P(None, "tp"),
            P(None, "tp"),
            P("tp", None),
            P(None, "tp"),
            P("tp", None),
        ),
        out_specs=(P(None, "seq", "tp"), P(None, None, "tp")),
        check_vma=False,
    )
```
